512 devices in a mesh: segment: 16 (over z, core), seq: 32 (over y, x).
Axes of the slice: x: 4, y: 8, z: 8, core: 2. Of those that a mesh axis runs over, the one named last changes fastest.
Arguments:
- features: bfloat16 [16, 4096, 4096], P('segment', 'seq'), may hold values from -6 to 6
- cotangent: bfloat16 [16, 4096, 4096], P('segment', 'seq'), may hold values from -6 to 6
- short_taps: float32 [16, 3, 3, 4096], P('segment'), may hold values from -3 to 3
- residue: float32 [16, 8, 4096], P('segment'), may hold values from -2 to 2
- decay_rates: float32 [16, 8, 4096], P('segment'), may hold values from 0.00024414062 to 0.05
- lengths: int32 [16, 8], P('segment'), may hold values from 1 to 2048, 4096 in all within a row
Outputs:
- passed: float32 [16, 4096, 4096], P('segment', 'seq')
The draws below stay inside these ranges and needn't reach their ends.
Inputs may be any that keep to these rules, and one draw needn't show every extreme that they name: Each section's 8 lengths sum to 4096, and the longest is exactly 2048.
All inputs are finite; a program needn't handle non-finite values.
Results may differ from the reference program's by a relative error of at most 0.0004.
Values may be sent and summed in bfloat16 or wider, within the bound.
A program may use at most 128 MiB of HBM per device.

```python
import math
import jax
import jax.numpy as jnp
import numpy as np
from jax import lax

TOK_DEV = 128
CHANNELS = 4096
POLES = 8
DOCS = 8
SEGMENTS = 16
TOKENS = 4096


def spread_log(unit, lower, upper):
    return jnp.exp(jnp.log(lower) + unit * (jnp.log(upper) - jnp.log(lower)))


def draw_decay_rates(key, part):
    key = jax.random.fold_in(key, 11)
    kind_key, value_key = jax.random.split(key)
    shape = (SEGMENTS, POLES, CHANNELS)
    picker = jax.random.uniform(kind_key, shape, jnp.float32)
    unit = jax.random.uniform(value_key, shape, jnp.float32)
    lowest = 1.0 / TOKENS
    highest = 6.4 / TOK_DEV
    slow_rates = spread_log(unit, lowest, 3.0 / TOKENS)
    middle_rates = spread_log(unit, 0.45 / TOK_DEV, 1.0 / TOK_DEV)
    fast_rates = spread_log(unit, 2.5 / TOK_DEV, highest)
    middle_share = 0.5
    slow_share = 0.25
    chosen = jnp.where(picker < middle_share, middle_rates, jnp.where(picker < middle_share + slow_share, slow_rates, fast_rates))
    return jnp.clip(chosen, lowest, highest).astype(jnp.float32)


def block_scale(own_key, dims, pieces, smallest, largest):
    gain, own = 1.0, jax.random.fold_in(own_key, 6)
    for dim, parts in pieces:
        steps = jnp.exp(jax.random.uniform(jax.random.fold_in(own, dim), (parts,), jnp.float32, smallest / len(pieces), largest / len(pieces)))
        gain = gain * jnp.repeat(steps, dims[dim] // parts).reshape([-1 if axis == dim else 1 for axis in range(len(dims))])
    return gain


def length_profile(amount, total, bound, skew):
    portions = [(1 << 20) // math.isqrt(rank ** skew) + 1 for rank in range(2, amount + 1)]
    spare, counts = total - bound - (amount - 1), [1] * (amount - 1)
    while spare > 0:
        movable = [i for i in range(amount - 1) if counts[i] < bound]
        whole, left = sum([portions[i] for i in movable]), spare
        for i in movable:
            addition = min(bound - counts[i], max(1, left * portions[i] // whole), spare)
            counts[i] = counts[i] + addition
            spare = spare - addition
    return np.array([bound] + counts)


def ragged(rng, amount, total, bound, lean):
    if amount == 2:
        one = jax.random.randint(rng, (), max(1, total - bound), min(bound, total - 1) + 1)
        return jnp.stack([one, total - one])
    sizes = jnp.asarray(length_profile(amount, total, bound, lean), jnp.int32)
    pairs = (amount - 1) // 2
    giver, taker = sizes[1:1 + 2 * pairs:2], sizes[2:2 + 2 * pairs:2]
    slack = jnp.minimum(giver - 1, bound - taker)
    shifted = jax.random.randint(jax.random.fold_in(rng, 1), (pairs,), 0, 1 << 20) % (slack + 1)
    sizes = sizes.at[1:1 + 2 * pairs:2].set(giver - shifted).at[2:2 + 2 * pairs:2].set(taker + shifted)
    return sizes[jax.random.permutation(jax.random.fold_in(rng, 2), amount)]


def scatter_about(own_key, shape, scale, reach, pieces=(), held_as=jnp.bfloat16):
    array = jax.random.normal(own_key, shape, jnp.float32) * scale
    if len(pieces) > 0:
        array = block_scale(own_key, shape, pieces, -0.22, 0.18) * array
    return jnp.clip(array, min=-reach, max=reach).astype(held_as)


def setup_inputs(seed: int = 0) -> dict:
    splits = jax.random.split(jax.random.key(seed), 7)
    return {
        "features": scatter_about(splits[0], (SEGMENTS, TOKENS, CHANNELS), 1.0, 6.0, ((0, 16), (1, 32))),
        "cotangent": scatter_about(splits[1], (SEGMENTS, TOKENS, CHANNELS), 1.0, 6.0, ((0, 16), (1, 32))),
        "short_taps": scatter_about(splits[2], (SEGMENTS, 3, 3, CHANNELS), 0.6, 3.0, ((0, 16),), jnp.float32),
        "residue": scatter_about(splits[3], (SEGMENTS, POLES, CHANNELS), POLES ** -0.5, 2.0, ((0, 16),), jnp.float32),
        "decay_rates": draw_decay_rates(jax.random.fold_in(splits[6], 71), 0),
        "lengths": jax.vmap(lambda own: ragged(own, DOCS, TOKENS, TOKENS // 2, 2))(jax.random.split(splits[5], SEGMENTS)).reshape((SEGMENTS, DOCS)).astype(jnp.int32),
    }


def shift_down(values, lag_steps, filler):
    padding = [(lag_steps, 0)] + [(0, 0)] * (values.ndim - 1)
    return jnp.pad(values, padding, constant_values=filler)[:values.shape[0]]

def shift_up(values, lag_steps, filler):
    padding = [(0, lag_steps)] + [(0, 0)] * (values.ndim - 1)
    return jnp.pad(values, padding, constant_values=filler)[lag_steps:]

def segment_gradient(operands):
    features, cotangent, short_taps, residue, decay_rates, lengths = operands
    residue = residue.T
    decay_rates = decay_rates.T
    doc_ends = jnp.cumsum(lengths).astype(jnp.int32)
    position = jnp.arange(TOKENS, dtype=jnp.int32)
    doc_ids = lax.optimization_barrier(jnp.sum((doc_ends[None, :] <= position[:, None]).astype(jnp.int32), axis=1)).astype(jnp.int32)
    inputs = features.astype(jnp.float32)
    grad_out = cotangent.astype(jnp.float32)
    streams = []
    for stream in range(3):
        summed = short_taps[stream, 0][None, :] * inputs
        for lag_steps in (1, 2):
            same_doc = (shift_down(doc_ids, lag_steps, -1) == doc_ids).astype(jnp.float32)[:, None]
            summed = summed + short_taps[stream, lag_steps][None, :] * same_doc * shift_down(inputs, lag_steps, 0.0)
        streams.append(summed)
    gate_stream, key_stream, value_stream = streams
    mixed_in = key_stream * value_stream
    decay = jnp.exp(-decay_rates)
    weights = residue * jnp.sqrt(2.0 * decay_rates)
    keep_prev = (shift_down(doc_ids, 1, -1) == doc_ids).astype(jnp.float32)
    keep_next = (shift_up(doc_ids, 1, -1) == doc_ids).astype(jnp.float32)

    def advance(state, item):
        row_input, keep_flag = item
        state = keep_flag * decay * state + row_input[:, None]
        return (state, lax.optimization_barrier(jnp.sum(weights * state, axis=1)))
    start_state = jnp.zeros(decay_rates.shape, jnp.float32)
    _, filtered = lax.scan(advance, start_state, (mixed_in, keep_prev))
    grad_filtered = grad_out * gate_stream
    grad_gate = grad_out * filtered
    _, grad_mixed = lax.scan(advance, start_state, (grad_filtered, keep_next), reverse=True)
    grad_key = grad_mixed * value_stream
    grad_value = grad_mixed * key_stream
    grads = (grad_gate, grad_key, grad_value)

    def tap_term(lag_steps):
        return sum((short_taps[stream, lag_steps][None, :] * grads[stream] for stream in range(3)))
    result = tap_term(0)
    for lag_steps in (1, 2):
        same_doc = (shift_up(doc_ids, lag_steps, -1) == doc_ids).astype(jnp.float32)[:, None]
        result = result + same_doc * shift_up(tap_term(lag_steps), lag_steps, 0.0)
    return result

def reference(features, cotangent, short_taps, residue, decay_rates, lengths):
    results = lax.map(segment_gradient, (features, cotangent, short_taps, residue, decay_rates, lengths))
    return jnp.roll(results, -1, axis=0)
```

```python
import jax
import jax.numpy as jnp
from jax import lax
from jax.experimental import pallas as pl
from jax.experimental.pallas import tpu as pltpu
from jax.sharding import PartitionSpec as P

MESH = pl.DeviceIdType.MESH
F32 = jnp.float32
TOK = 128
HALO = 2
LANES = 128
GROUP = 8
WIDTH = GROUP * LANES
PARTS = 4
POLES = 8
DOCS = 8
ROWS = 8
XS = TOK + 2 * HALO
ES = TOK + HALO
STATE = POLES * GROUP
TOP = 32767.0


def tile(ref, i):
    return ref[pl.ds(pl.multiple_of(i * GROUP, GROUP), GROUP), :]


def put(ref, i, value):
    ref[pl.ds(pl.multiple_of(i * GROUP, GROUP), GROUP), :] = value


def total_of(values):
    values = list(values)
    while len(values) > 1:
        values = [a + b for a, b in zip(values[::2], values[1::2])] + (
            [values[-1]] if len(values) % 2 else []
        )
    return values[0]


def mixer_kernel(
    feat, cot, taps, res, rates, lens, out_q, out_s,
    feat_v, cot_v, taps_v, res_v, rates_v,
    xt, gt, kt, vt, gft, ft, ot, k1, k2, mt, mh,
    tap_t, dec, wts, dd, dd4,
    tails, row_in, sums, col_in, sent, inc, qv, sv, iv,
    load_sem, par_sem, halo_send, halo_recv, tail_send, tail_recv,
    col_send, col_recv, inc_send, inc_recv, out_send, out_recv,
):
    sg = lax.axis_index("segment")
    q = lax.axis_index("seq")
    n_sg = lax.axis_size("segment")
    n_q = lax.axis_size("seq")
    y, x = q // PARTS, q % PARTS
    before, after = (q + n_q - 1) % n_q, (q + 1) % n_q
    sg_to, sg_from = (sg + n_sg - 1) % n_sg, (sg + 1) % n_sg

    def row_mate(k):
        return y * PARTS + (x + k) % PARTS

    def col_mate(k):
        return ((y + k) % ROWS) * PARTS + x

    loads = []
    for c in range(PARTS):
        cols = pl.ds(c * WIDTH, WIDTH)
        loads.append((
            pltpu.make_async_copy(feat.at[0, :, cols], feat_v.at[c], load_sem.at[0, c]),
            pltpu.make_async_copy(cot.at[0, :, cols], cot_v.at[c], load_sem.at[1, c]),
        ))
    pars = [
        pltpu.make_async_copy(taps.at[0], taps_v, par_sem.at[0]),
        pltpu.make_async_copy(res.at[0], res_v, par_sem.at[1]),
        pltpu.make_async_copy(rates.at[0], rates_v, par_sem.at[2]),
    ]
    for copy in loads[0]:
        copy.start()
    for copy in pars:
        copy.start()
    for pair in loads[1:]:
        for copy in pair:
            copy.start()

    barrier = pltpu.get_barrier_semaphore()

    def greet(**where):
        pl.semaphore_signal(barrier, inc=1, device_id=where, device_id_type=MESH)

    for k in range(1, PARTS):
        greet(seq=row_mate(k))
    for k in range(1, ROWS):
        greet(seq=col_mate(k))
    greet(seq=before)
    greet(seq=after)
    greet(segment=sg_to)
    greet(segment=sg_from)

    ends = []
    run = jnp.int32(0)
    for i in range(DOCS):
        run = run + lens[0, i]
        ends.append(jnp.full((GROUP, LANES), run, jnp.int32))

    def doc_at(position):
        spot = jnp.full((GROUP, LANES), position, jnp.int32)
        count = total_of([jnp.where(end <= spot, 1, 0) for end in ends])
        return jnp.where(spot < 0, -1, count)

    def same(a, b):
        return jnp.where(a == b, 1.0, 0.0).astype(F32)

    first = q * TOK
    doc_tail = doc_at(first + TOK - 1)
    doc_head = doc_at(first + HALO)

    def mask_step(e, carry):
        d1, d2 = carry
        d0 = doc_at(first + e)
        put(k1, e, same(d0, d1))
        put(k2, e, same(d0, d2))
        put(mt, e, same(d0, doc_tail))
        put(mh, e, same(d0, doc_head))
        return d0, d1

    lax.fori_loop(0, XS, mask_step, (doc_at(first - 1), doc_at(first - 2)))

    for copy in pars:
        copy.wait()
    for c in range(PARTS):
        for g in range(GROUP):
            cols = slice(c * WIDTH + g * LANES, c * WIDTH + (g + 1) * LANES)
            rate = rates_v[:, cols]
            spread = pl.ds(c * STATE + g, POLES, stride=GROUP)
            dec[spread, :] = jnp.exp(-rate)
            dd[spread, :] = jnp.exp(-rate * float(TOK))
            dd4[spread, :] = jnp.exp(-rate * float(TOK * PARTS))
            wts[spread, :] = res_v[:, cols] * jnp.sqrt(2.0 * rate)
            for stream in range(3):
                for lag in range(3):
                    row = (c * 9 + stream * 3 + lag) * GROUP + g
                    tap_t[row : row + 1, :] = taps_v[stream, lag : lag + 1, cols]

    def relay(c, _):
        for which, (source, target, slots, shift) in enumerate(
            ((feat_v, xt, XS, HALO), (cot_v, gt, ES, 0))
        ):
            pltpu.make_async_copy(
                (feat, cot)[which].at[0, :, pl.ds(0, WIDTH)], source.at[c], load_sem.at[which, c]
            ).wait()

            def rows(t, _):
                for g in range(GROUP):
                    value = source[
                        c, pl.ds(pl.multiple_of(t * 16, 16), 16), g * LANES : (g + 1) * LANES
                    ].astype(F32)
                    target[
                        pl.ds((c * slots + shift + t * 16) * GROUP + g, 16, stride=GROUP), :
                    ] = value
                return 0

            lax.fori_loop(0, TOK // 16, rows, 0)
        return 0

    def halo_copies(c):
        def spot(ref, slots, at):
            return ref.at[pl.ds(pl.multiple_of((c * slots + at) * GROUP, GROUP), HALO * GROUP), :]

        return [
            pltpu.make_async_remote_copy(
                src_ref=spot(ref, slots, here),
                dst_ref=spot(ref, slots, there),
                send_sem=halo_send.at[c, n],
                recv_sem=halo_recv.at[c, n],
                device_id={"seq": to},
                device_id_type=MESH,
            )
            for n, (ref, slots, here, there, to) in enumerate((
                (xt, XS, TOK, 0, after),
                (xt, XS, HALO, TOK + HALO, before),
                (gt, ES, 0, TOK, before),
            ))
        ]

    lax.fori_loop(0, 1, relay, 0)
    pl.semaphore_wait(barrier, (PARTS - 1) + (ROWS - 1) + 4)

    def send_halo(c, _):
        for copy in halo_copies(c):
            copy.start()
        return 0

    send_halo(0, 0)

    def relay_and_send(c, _):
        relay(c, 0)
        send_halo(c, 0)
        return 0

    lax.fori_loop(1, PARTS, relay_and_send, 0)

    def tail_copy(c):
        return pltpu.make_async_remote_copy(
            src_ref=tails.at[pl.ds(pl.multiple_of(c * 2 * STATE, 8), 2 * STATE), :],
            dst_ref=row_in.at[pl.ds(pl.multiple_of(x * 2 * STATE, 8), 2 * STATE), :],
            send_sem=tail_send.at[c],
            recv_sem=tail_recv.at[x],
            device_id={"seq": y * PARTS + c},
            device_id_type=MESH,
        )

    def first_pass(c, _):
        for copy in halo_copies(c):
            copy.wait_recv()
        tap = [tile(tap_t, c * 9 + n) for n in range(9)]
        x_at, e_at = c * XS, c * ES

        def streams(i, carry):
            x1, x2 = carry
            for u in range(5):
                e = i * 5 + u
                x0 = tile(xt, x_at + HALO + e)
                a, b = x1 * tile(k1, e), x2 * tile(k2, e)
                gate, key, value = (
                    tap[3 * n] * x0 + tap[3 * n + 1] * a + tap[3 * n + 2] * b for n in range(3)
                )
                put(kt, e_at + e, key)
                put(vt, e_at + e, value)
                put(gft, e_at + e, tile(gt, e_at + e) * gate)
                x1, x2 = x0, x1
            return x1, x2

        lax.fori_loop(0, ES // 5, streams, (tile(xt, x_at + 1), tile(xt, x_at)))

        decay = [tile(dec, c * POLES + p) for p in range(POLES)]

        def ends_step(i, carry):
            fwd, bwd = carry
            for u in range(4):
                e = i * 4 + u
                r = ES - 1 - e
                mixed = tile(kt, e_at + e) * tile(vt, e_at + e) * tile(mt, e)
                grad = tile(gft, e_at + r) * tile(mh, r)
                fwd = tuple(d * s + mixed for d, s in zip(decay, fwd))
                bwd = tuple(d * s + grad for d, s in zip(decay, bwd))
            return fwd, bwd

        zero = tuple(jnp.zeros((GROUP, LANES), F32) for _ in range(POLES))
        fwd, bwd = lax.fori_loop(0, TOK // 4, ends_step, (zero, zero))
        for p in range(POLES):
            put(tails, c * 2 * POLES + p, fwd[p])
            put(tails, c * 2 * POLES + POLES + p, bwd[p])

        @pl.when(c != x)
        def _():
            tail_copy(c).start()

        @pl.when(c == x)
        def _():
            for p in range(2 * POLES):
                put(row_in, x * 2 * POLES + p, tile(tails, c * 2 * POLES + p))

        return 0

    lax.fori_loop(0, PARTS, first_pass, 0)

    for k in range(1, PARTS):
        other = (x + k) % PARTS
        pltpu.make_async_remote_copy(
            src_ref=tails.at[pl.ds(0, 2 * STATE), :],
            dst_ref=row_in.at[pl.ds(pl.multiple_of(other * 2 * STATE, 8), 2 * STATE), :],
            send_sem=tail_send.at[other],
            recv_sem=tail_recv.at[other],
            device_id={"seq": row_mate(k)},
            device_id_type=MESH,
        ).wait_recv()

    row_first = y * PARTS * TOK
    fwd_docs = [doc_at(row_first + n * TOK - 1) for n in range(PARTS + 1)]
    bwd_docs = [doc_at(row_first + n * TOK + HALO) for n in range(PARTS + 1)]
    fwd_link = [same(fwd_docs[n], fwd_docs[n + 1]) for n in range(PARTS)]
    bwd_link = [same(bwd_docs[n], bwd_docs[n + 1]) for n in range(PARTS)]

    def row_total(p, _):
        span = tile(dd, x * POLES + p)
        forward = tile(row_in, p)
        for n in range(1, PARTS):
            forward = tile(row_in, n * 2 * POLES + p) + fwd_link[n] * span * forward
        put(sums, p, forward)
        backward = tile(row_in, (PARTS - 1) * 2 * POLES + POLES + p)
        for n in range(PARTS - 2, -1, -1):
            backward = tile(row_in, n * 2 * POLES + POLES + p) + bwd_link[n] * span * backward
        put(sums, POLES + p, backward)
        return 0

    lax.fori_loop(0, POLES, row_total, 0)

    def col_copy(way, k):
        slot = way * PARTS + k - 1
        return pltpu.make_async_remote_copy(
            src_ref=sums.at[pl.ds(way * STATE, STATE), :],
            dst_ref=col_in.at[pl.ds(slot * STATE, STATE), :],
            send_sem=col_send.at[slot],
            recv_sem=col_recv.at[slot],
            device_id={"seq": col_mate(k if way == 0 else ROWS - k)},
            device_id_type=MESH,
        )

    reach = 4
    for k in range(1, reach + 1):
        for way in range(2):
            col_copy(way, k).start()

    row_span = TOK * PARTS
    past = [doc_at(row_first - k * row_span - 1) for k in range(0, reach)]
    coming = [doc_at(row_first + k * row_span + HALO) for k in range(1, reach + 1)]
    past_link = [same(past[n], past[n + 1]) for n in range(reach - 1)]
    coming_link = [same(coming[n], coming[n + 1]) for n in range(reach - 1)]

    for k in range(1, reach + 1):
        for way in range(2):
            col_copy(way, k).wait_recv()

    def entering(p, _):
        span, long_span = tile(dd, x * POLES + p), tile(dd4, x * POLES + p)
        for way, links in ((0, past_link), (1, coming_link)):
            state = tile(col_in, (way * PARTS + reach - 1) * POLES + p)
            for k in range(reach - 1, 0, -1):
                state = (
                    tile(col_in, (way * PARTS + k - 1) * POLES + p)
                    + links[k - 1] * long_span * state
                )
            order = range(PARTS) if way == 0 else range(PARTS - 1, -1, -1)
            for n in order:
                put(sent, n * 2 * POLES + way * POLES + p, state)
                link = fwd_link[n] if way == 0 else bwd_link[n]
                own = tile(row_in, n * 2 * POLES + way * POLES + p)
                state = own + link * span * state
        return 0

    lax.fori_loop(0, POLES, entering, 0)

    def inc_copy(k):
        other = (x + k) % PARTS
        return pltpu.make_async_remote_copy(
            src_ref=sent.at[pl.ds(pl.multiple_of(other * 2 * STATE, 8), 2 * STATE), :],
            dst_ref=inc.at[pl.ds(pl.multiple_of(x * 2 * STATE, 8), 2 * STATE), :],
            send_sem=inc_send.at[other],
            recv_sem=inc_recv.at[x],
            device_id={"seq": row_mate(k)},
            device_id_type=MESH,
        )

    for k in range(1, PARTS):
        inc_copy(k).start()
    for p in range(2 * POLES):
        put(inc, x * 2 * POLES + p, tile(sent, x * 2 * POLES + p))

    def out_copies(c):
        cols = pl.ds(pl.multiple_of(c * WIDTH, WIDTH), WIDTH)
        scale_rows = pl.ds(pl.multiple_of(c * GROUP, GROUP), GROUP)
        return [
            pltpu.make_async_remote_copy(
                src_ref=source,
                dst_ref=target,
                send_sem=out_send.at[n, c],
                recv_sem=out_recv.at[n, c],
                device_id={"segment": sg_to},
                device_id_type=MESH,
            )
            for n, (source, target) in enumerate((
                (qv.at[c], out_q.at[:, cols]),
                (sv.at[scale_rows, :], out_s.at[scale_rows, :]),
            ))
        ]

    def second_pass(step, _):
        c = (x + step) % PARTS

        @pl.when(step > 0)
        def _():
            pltpu.make_async_remote_copy(
                src_ref=sent.at[pl.ds(0, 2 * STATE), :],
                dst_ref=inc.at[pl.ds(pl.multiple_of(c * 2 * STATE, 8), 2 * STATE), :],
                send_sem=inc_send.at[c],
                recv_sem=inc_recv.at[c],
                device_id={"seq": y * PARTS + c},
                device_id_type=MESH,
            ).wait_recv()

        e_at = c * ES
        decay = [tile(dec, c * POLES + p) for p in range(POLES)]
        weight = [tile(wts, c * POLES + p) for p in range(POLES)]

        def forward(i, state):
            for u in range(5):
                e = i * 5 + u
                mixed = tile(kt, e_at + e) * tile(vt, e_at + e)
                keep = tile(k1, e)
                state = tuple((keep * d) * s + mixed for d, s in zip(decay, state))
                filtered = total_of([w * s for w, s in zip(weight, state)])
                put(ft, e, filtered * tile(gt, e_at + e))
            return state

        lax.fori_loop(
            0, ES // 5, forward, tuple(tile(inc, c * 2 * POLES + p) for p in range(POLES))
        )
        tap = [tile(tap_t, c * 9 + n) for n in range(9)]

        def back_step(e, carry):
            state, t1, t2, t22, most = carry
            grad = tile(gft, e_at + e)
            keep, skip = tile(k1, e + 1), tile(k2, e + 2)
            state = tuple((keep * d) * s + grad for d, s in zip(decay, state))
            mixed = total_of([w * s for w, s in zip(weight, state)])
            grads = (tile(ft, e), mixed * tile(vt, e_at + e), mixed * tile(kt, e_at + e))
            terms = [
                tap[lag] * grads[0] + tap[3 + lag] * grads[1] + tap[6 + lag] * grads[2]
                for lag in range(3)
            ]
            result = terms[0] + keep * t1 + skip * t22
            return result, (state, terms[1], terms[2], t2, most)

        nothing = jnp.zeros((GROUP, LANES), F32)
        carry = (
            tuple(tile(inc, c * 2 * POLES + POLES + p) for p in range(POLES)),
            nothing, nothing, nothing, nothing,
        )
        for e in (TOK + 1, TOK):
            _, carry = back_step(e, carry)

        def backward(i, carry):
            for u in range(4):
                e = TOK - 1 - (i * 4 + u)
                result, (state, t1, t2, t22, most) = back_step(e, carry)
                put(ot, e, result)
                carry = (state, t1, t2, t22, jnp.maximum(most, jnp.abs(result)))
            return carry

        carry = lax.fori_loop(0, TOK // 4, backward, carry)
        most = jnp.maximum(carry[4], 1e-30)
        put(sv, c, most * (1.0 / TOP))
        iv[...] = TOP / most

        def coded(t, _):
            for g in range(GROUP):
                value = ot[pl.ds(t * 16 * GROUP + g, 16, stride=GROUP), :] * iv[g : g + 1, :]
                qv[c, pl.ds(pl.multiple_of(t * 16, 16), 16), g * LANES : (g + 1) * LANES] = (
                    jnp.round(value).astype(jnp.int32).astype(jnp.int16)
                )
            return 0

        lax.fori_loop(0, TOK // 16, coded, 0)
        for copy in out_copies(c):
            copy.start()
        return 0

    lax.fori_loop(0, PARTS, second_pass, 0)

    def finish(c, _):
        for copy in halo_copies(c):
            copy.wait_send()

        @pl.when(c != x)
        def _():
            tail_copy(c).wait_send()

        for copy in out_copies(c):
            copy.wait()
        return 0

    lax.fori_loop(0, PARTS, finish, 0)
    for k in range(1, reach + 1):
        for way in range(2):
            col_copy(way, k).wait_send()
    for k in range(1, PARTS):
        inc_copy(k).wait_send()


def shards(features, cotangent, short_taps, residue, decay_rates, lengths):
    tokens, channels = features.shape[1:]
    any_space = pl.BlockSpec(memory_space=pl.ANY)
    bf16 = jnp.bfloat16
    vm = pltpu.VMEM
    dma = pltpu.SemaphoreType.DMA
    whole = lambda rows: vm((rows * GROUP, LANES), F32)
    coded, scale = pl.pallas_call(
        mixer_kernel,
        out_shape=(
            jax.ShapeDtypeStruct((tokens, channels), jnp.int16),
            jax.ShapeDtypeStruct((PARTS * GROUP, LANES), F32),
        ),
        in_specs=[any_space] * 5 + [pl.BlockSpec(memory_space=pltpu.SMEM)],
        out_specs=(any_space, any_space),
        scratch_shapes=[
            vm((PARTS, TOK, WIDTH), bf16), vm((PARTS, TOK, WIDTH), bf16),
            vm((3, 3, channels), F32), vm((POLES, channels), F32), vm((POLES, channels), F32),
            whole(PARTS * XS), whole(PARTS * ES), whole(PARTS * ES), whole(PARTS * ES),
            whole(PARTS * ES), whole(ES), whole(ES),
            whole(XS), whole(XS), whole(XS), whole(XS),
            whole(PARTS * 9), whole(PARTS * POLES), whole(PARTS * POLES),
            whole(PARTS * POLES), whole(PARTS * POLES),
            whole(PARTS * 2 * POLES), whole(PARTS * 2 * POLES), whole(2 * POLES),
            whole(2 * PARTS * POLES), whole(PARTS * 2 * POLES), whole(PARTS * 2 * POLES),
            vm((PARTS, TOK, WIDTH), jnp.int16), whole(PARTS), whole(1),
            dma((2, PARTS)), dma((3,)), dma((PARTS, 3)), dma((PARTS, 3)),
            dma((PARTS,)), dma((PARTS,)), dma((2 * PARTS,)), dma((2 * PARTS,)),
            dma((PARTS,)), dma((PARTS,)), dma((2, PARTS)), dma((2, PARTS)),
        ],
        compiler_params=pltpu.CompilerParams(
            collective_id=0, has_side_effects=True, vmem_limit_bytes=40 * 1024 * 1024
        ),
        cost_estimate=pl.CostEstimate(
            flops=160 * tokens * channels, bytes_accessed=8 * tokens * channels, transcendentals=0
        ),
    )(features, cotangent, short_taps, residue, decay_rates, lengths)
    return (coded.astype(F32) * scale.reshape(1, channels))[None]


def solution(mesh):
    in_specs = (
        P("segment", "seq", None),
        P("segment", "seq", None),
        P("segment", None, None, None),
        P("segment", None, None),
        P("segment", None, None),
        P("segment", None),
    )
    out_specs = P("segment", "seq", None)
    return jax.shard_map(shards, mesh=mesh, in_specs=in_specs, out_specs=out_specs, check_vma=False)
```

```python
import jax
import jax.numpy as jnp
from jax import lax
from jax.experimental import pallas as pl
from jax.experimental.pallas import tpu as pltpu
from jax.sharding import PartitionSpec as P

MESH = pl.DeviceIdType.MESH
F32 = jnp.float32
TOK = 128
HALO = 2
LANES = 128
GROUP = 8
WIDTH = GROUP * LANES
PARTS = 4
POLES = 8
DOCS = 8
ROWS = 8
REACH = 4
XS = TOK + 2 * HALO
ES = TOK + HALO
HALF = TOK // 2
STATE = POLES * GROUP
PAIR = POLES // PARTS
CELL = 2 * PAIR
TOP = 32767.0


def tile(ref, i):
    return ref[pl.ds(pl.multiple_of(i * GROUP, GROUP), GROUP), :]


def put(ref, i, value):
    ref[pl.ds(pl.multiple_of(i * GROUP, GROUP), GROUP), :] = value


def total_of(values):
    values = list(values)
    while len(values) > 1:
        values = [a + b for a, b in zip(values[::2], values[1::2])] + (
            [values[-1]] if len(values) % 2 else []
        )
    return values[0]


def mixer_kernel(
    feat, cot, taps, res, rates, lens, out_q, out_late, out_early,
    feat_v, cot_v, feat_e, cot_e, res_v, rates_v,
    xt, gt, kt, vt, gft, ft, mx, ot, k1, k2, mt, mh, mi, mo,
    tap_t, dec, wts, near, past, grow, dd, dd4,
    tails, row_in, sums, col_in, sent, inc, row_link, col_link, qv, sv, iv,
    load_sem, par_sem, halo_send, halo_recv, tail_send, tail_recv,
    col_send, col_recv, inc_send, inc_recv, out_send, out_recv, rim_sem,
):
    sg = lax.axis_index("segment")
    q = lax.axis_index("seq")
    n_sg = lax.axis_size("segment")
    n_q = lax.axis_size("seq")
    y, x = q // PARTS, q % PARTS
    before, after = (q + n_q - 1) % n_q, (q + 1) % n_q
    sg_to, sg_from = (sg + n_sg - 1) % n_sg, (sg + 1) % n_sg

    def row_mate(k):
        return y * PARTS + (x + k) % PARTS

    def col_mate(k):
        return ((y + k) % ROWS) * PARTS + x

    loads = []
    for c in range(PARTS):
        cols = pl.ds(c * WIDTH, WIDTH)
        loads.append((
            pltpu.make_async_copy(feat.at[0, :, cols], feat_v.at[c], load_sem.at[0, c]),
            pltpu.make_async_copy(cot.at[0, :, cols], cot_v.at[c], load_sem.at[1, c]),
        ))
    pars = [
        pltpu.make_async_copy(taps, tap_t, par_sem.at[0]),
        pltpu.make_async_copy(res.at[0], res_v, par_sem.at[1]),
        pltpu.make_async_copy(rates.at[0], rates_v, par_sem.at[2]),
    ]
    rim = [
        pltpu.make_async_copy(feat.at[0, pl.ds(0, 16), :], feat_e.at[0], rim_sem.at[0]),
        pltpu.make_async_copy(feat.at[0, pl.ds(TOK - 16, 16), :], feat_e.at[1], rim_sem.at[1]),
        pltpu.make_async_copy(cot.at[0, pl.ds(0, 16), :], cot_e, rim_sem.at[2]),
    ]
    for copy in rim:
        copy.start()
    for copy in loads[0]:
        copy.start()
    for copy in pars:
        copy.start()
    for pair in loads[1:]:
        for copy in pair:
            copy.start()

    barrier = pltpu.get_barrier_semaphore()

    def greet(**where):
        pl.semaphore_signal(barrier, inc=1, device_id=where, device_id_type=MESH)

    for k in range(1, PARTS):
        greet(seq=row_mate(k))
    for k in range(1, ROWS):
        greet(seq=col_mate(k))
    greet(seq=before)
    greet(seq=after)
    greet(segment=sg_to)
    greet(segment=sg_from)

    ends = []
    run = jnp.int32(0)
    for i in range(DOCS):
        run = run + lens[0, i]
        ends.append(jnp.full((GROUP, LANES), run, jnp.int32))

    def doc_at(position):
        spot = jnp.full((GROUP, LANES), position, jnp.int32)
        count = total_of([jnp.where(end <= spot, 1, 0) for end in ends])
        return jnp.where(spot < 0, -1, count)

    def same(a, b):
        return jnp.where(a == b, 1.0, 0.0).astype(F32)

    first = q * TOK
    doc_tail = doc_at(first + TOK - 1)
    doc_head = doc_at(first + HALO)
    doc_in = doc_at(first - 1)
    doc_out = doc_at(first + ES)

    def mask_step(e, carry):
        d1, d2 = carry
        d0 = doc_at(first + e)
        put(k1, e, same(d0, d1))
        put(k2, e, same(d0, d2))
        put(mt, e, same(d0, doc_tail))
        put(mh, e, same(d0, doc_head))
        put(mi, e, same(d0, doc_in))
        put(mo, e, same(d0, doc_out))
        return d0, d1

    lax.fori_loop(0, XS, mask_step, (doc_at(first - 1), doc_at(first - 2)))

    def relay(c):
        for which, (far, near_v) in enumerate(((feat, feat_v), (cot, cot_v))):
            pltpu.make_async_copy(
                far.at[0, :, pl.ds(0, WIDTH)], near_v.at[c], load_sem.at[which, c]
            ).wait()

        def rows(t, _):
            for source, target, shift in ((feat_v, xt, HALO), (cot_v, gt, 0)):
                for g in range(GROUP):
                    value = source[
                        c, pl.ds(pl.multiple_of(t * 16, 16), 16), g * LANES : (g + 1) * LANES
                    ].astype(F32)
                    target[c, pl.ds((shift + t * 16) * GROUP + g, 16, stride=GROUP), :] = value
            return 0

        lax.fori_loop(1, TOK // 16 - 1, rows, 0)
        t = TOK // 16 - 1
        for g in range(GROUP):
            value = cot_v[c, t * 16 : TOK, g * LANES : (g + 1) * LANES].astype(F32)
            gt[c, pl.ds(t * 16 * GROUP + g, 16, stride=GROUP), :] = value

    halo_copies = [
        pltpu.make_async_remote_copy(
            src_ref=ref.at[:, pl.ds(here * GROUP, HALO * GROUP), :],
            dst_ref=ref.at[:, pl.ds(there * GROUP, HALO * GROUP), :],
            send_sem=halo_send.at[n],
            recv_sem=halo_recv.at[n],
            device_id={"seq": to},
            device_id_type=MESH,
        )
        for n, (ref, here, there, to) in enumerate((
            (xt, TOK, 0, after),
            (xt, HALO, TOK + HALO, before),
            (gt, 0, TOK, before),
        ))
    ]

    for copy in rim:
        copy.wait()
    for c in range(PARTS):
        for g in range(GROUP):
            cols = slice(c * WIDTH + g * LANES, c * WIDTH + (g + 1) * LANES)
            spread = pl.ds(HALO * GROUP + g, 16, stride=GROUP)
            xt[c, spread, :] = feat_e[0, :, cols].astype(F32)
            spread = pl.ds((HALO + TOK - 16) * GROUP + g, 16, stride=GROUP)
            xt[c, spread, :] = feat_e[1, :, cols].astype(F32)
            gt[c, pl.ds(g, 16, stride=GROUP), :] = cot_e[:, cols].astype(F32)
    pl.semaphore_wait(barrier, (PARTS - 1) + (ROWS - 1) + 4)
    for copy in halo_copies:
        copy.start()

    for copy in pars:
        copy.wait()
    for c in range(PARTS):
        for g in range(GROUP):
            cols = slice(c * WIDTH + g * LANES, c * WIDTH + (g + 1) * LANES)
            rate = rates_v[:, cols]
            spread = pl.ds(c * STATE + g, POLES, stride=GROUP)
            dec[spread, :] = jnp.exp(-rate)
            near[spread, :] = jnp.exp(-rate * float(TOK - HALO))
            past[spread, :] = jnp.exp(-rate * float(ES))
            grow[spread, :] = jnp.exp(rate)
            dd[spread, :] = jnp.exp(-rate * float(TOK))
            dd4[spread, :] = jnp.exp(-rate * float(TOK * PARTS))
            wts[spread, :] = res_v[:, cols] * jnp.sqrt(2.0 * rate)

    def cells(ref, at, count=CELL):
        return ref.at[pl.ds(pl.multiple_of(at * GROUP, GROUP), count * GROUP), :]

    def cell(c, who, way, pole):
        return ((c * PARTS + who) * 2 + way) * PAIR + pole

    def tail_copy(c, k):
        other = (x + k) % PARTS
        return pltpu.make_async_remote_copy(
            src_ref=cells(tails, cell(c, other, 0, 0)),
            dst_ref=cells(row_in, cell(c, x, 0, 0)),
            send_sem=tail_send.at[c, k],
            recv_sem=tail_recv.at[c, k],
            device_id={"seq": row_mate(k)},
            device_id_type=MESH,
        )

    def col_copy(c, way, k):
        slot = way * REACH + k - 1
        return pltpu.make_async_remote_copy(
            src_ref=cells(sums, (c * 2 + way) * PAIR, PAIR),
            dst_ref=cells(col_in, (c * 2 * REACH + slot) * PAIR, PAIR),
            send_sem=col_send.at[c, slot],
            recv_sem=col_recv.at[c, slot],
            device_id={"seq": col_mate(k if way == 0 else ROWS - k)},
            device_id_type=MESH,
        )

    def inc_copy(c, k):
        other = (x + k) % PARTS
        return pltpu.make_async_remote_copy(
            src_ref=cells(sent, cell(c, other, 0, 0)),
            dst_ref=cells(inc, cell(c, x, 0, 0)),
            send_sem=inc_send.at[c, k],
            recv_sem=inc_recv.at[c, k],
            device_id={"seq": row_mate(k)},
            device_id_type=MESH,
        )

    row_first = y * PARTS * TOK
    row_span = TOK * PARTS

    def row_links():
        fwd = [doc_at(row_first + n * TOK - 1) for n in range(PARTS + 1)]
        bwd = [doc_at(row_first + n * TOK + HALO) for n in range(PARTS + 1)]
        return [[same(docs[n], docs[n + 1]) for n in range(PARTS)] for docs in (fwd, bwd)]

    def col_links():
        gone = [doc_at(row_first - k * row_span - 1) for k in range(REACH)]
        coming = [doc_at(row_first + k * row_span + HALO) for k in range(1, REACH + 1)]
        return [[same(docs[n], docs[n + 1]) for n in range(REACH - 1)] for docs in (gone, coming)]

    for way, links in enumerate(row_links()):
        for n, link in enumerate(links):
            put(row_link, way * PARTS + n, link)
    for way, links in enumerate(col_links()):
        for n, link in enumerate(links):
            put(col_link, way * PARTS + n, link)

    def along_row(c):
        for k in range(1, PARTS):
            tail_copy(c, k).wait_recv()
        for pole in range(PAIR):
            span = tile(dd, c * POLES + x * PAIR + pole)
            for way in range(2):
                order = list(range(PARTS)) if way == 0 else list(range(PARTS - 1, -1, -1))
                state = tile(row_in, cell(c, order[0], way, pole))
                for n in order[1:]:
                    link = tile(row_link, way * PARTS + n)
                    state = tile(row_in, cell(c, n, way, pole)) + link * span * state
                put(sums, (c * 2 + way) * PAIR + pole, state)
        for k in range(1, REACH + 1):
            for way in range(2):
                col_copy(c, way, k).start()

    def entering(c):
        for k in range(1, REACH + 1):
            for way in range(2):
                col_copy(c, way, k).wait_recv()
        for pole in range(PAIR):
            at = c * POLES + x * PAIR + pole
            span, long_span = tile(dd, at), tile(dd4, at)
            for way in range(2):
                slot = (c * 2 + way) * REACH
                state = tile(col_in, (slot + REACH - 1) * PAIR + pole)
                for k in range(REACH - 1, 0, -1):
                    link = tile(col_link, way * PARTS + k - 1)
                    state = tile(col_in, (slot + k - 1) * PAIR + pole) + link * long_span * state
                order = range(PARTS) if way == 0 else range(PARTS - 1, -1, -1)
                for n in order:
                    put(sent, cell(c, n, way, pole), state)
                    link = tile(row_link, way * PARTS + n)
                    state = tile(row_in, cell(c, n, way, pole)) + link * span * state
        for k in range(1, PARTS):
            inc_copy(c, k).start()
        for n in range(CELL):
            put(inc, cell(c, x, 0, n), tile(sent, cell(c, x, 0, n)))

    def xtile(c, slot):
        return xt[c, pl.ds(pl.multiple_of(slot * GROUP, GROUP), GROUP), :]

    def gtile(c, e):
        return gt[c, pl.ds(pl.multiple_of(e * GROUP, GROUP), GROUP), :]

    def first_pass(c, _):
        relay(c)
        tap = [tap_t[n, pl.ds(pl.multiple_of(c * GROUP, GROUP), GROUP), :] for n in range(9)]
        e_at = c * ES

        def stream(e, x1, x2):
            x0 = xtile(c, HALO + e)
            a, b = x1 * tile(k1, e), x2 * tile(k2, e)
            gate, key, value = (
                tap[3 * n] * x0 + tap[3 * n + 1] * a + tap[3 * n + 2] * b for n in range(3)
            )
            grad = gtile(c, e) * gate
            put(kt, e_at + e, key)
            put(vt, e_at + e, value)
            put(gft, e_at + e, grad)
            return x0, key * value, grad

        def streams(i, carry):
            x1, x2 = carry
            for u in range(6):
                x0, _, _ = stream(HALO + i * 6 + u, x1, x2)
                x1, x2 = x0, x1
            return x1, x2

        inner = TOK - HALO
        lax.fori_loop(0, inner // 6, streams, (xtile(c, HALO + 1), xtile(c, HALO)))

        decay = [tile(dec, c * POLES + p) for p in range(POLES)]

        def ends_step(i, carry):
            fwd, bwd = carry
            for u in range(3):
                e = HALO + i * 3 + u
                r = TOK - 1 - (i * 3 + u)
                mixed = tile(kt, e_at + e) * tile(vt, e_at + e) * tile(mt, e)
                grad = tile(gft, e_at + r) * tile(mh, r)
                fwd = tuple(d * s + mixed for d, s in zip(decay, fwd))
                bwd = tuple(d * s + grad for d, s in zip(decay, bwd))
            return fwd, bwd

        zero = tuple(jnp.zeros((GROUP, LANES), F32) for _ in range(POLES))
        fwd, bwd = lax.fori_loop(0, inner // 3, ends_step, (zero, zero))

        @pl.when(c == 0)
        def _():
            for copy in halo_copies:
                copy.wait_recv()

        x0, mixed0, _ = stream(0, xtile(c, 1), xtile(c, 0))
        _, mixed1, _ = stream(1, x0, xtile(c, 1))
        x0, _, grad0 = stream(TOK, xtile(c, TOK + 1), xtile(c, TOK))
        _, _, grad1 = stream(TOK + 1, x0, xtile(c, TOK + 1))
        mixed0, mixed1 = mixed0 * tile(mt, 0), mixed1 * tile(mt, 1)
        grad0, grad1 = grad0 * tile(mh, TOK), grad1 * tile(mh, TOK + 1)
        for p in range(POLES):
            far = tile(near, c * POLES + p)
            at = (c, p // PAIR)
            put(tails, cell(*at, 0, p % PAIR), fwd[p] + far * (decay[p] * mixed0 + mixed1))
            put(tails, cell(*at, 1, p % PAIR), bwd[p] + far * (decay[p] * grad1 + grad0))
        for k in range(1, PARTS):
            tail_copy(c, k).start()
        for n in range(CELL):
            put(row_in, cell(c, x, 0, n), tile(tails, cell(c, x, 0, n)))

        @pl.when(c >= 2)
        def _():
            along_row(c - 2)

        return 0

    lax.fori_loop(0, PARTS, first_pass, 0)

    def own_filters(c, _):
        e_at = c * ES
        decay = [tile(dec, c * POLES + p) for p in range(POLES)]
        weight = [tile(wts, c * POLES + p) for p in range(POLES)]

        def both(i, carry):
            fwd, bwd = carry
            for u in range(5):
                e = i * 5 + u
                r = ES - 1 - e
                mixed = tile(kt, e_at + e) * tile(vt, e_at + e)
                grad = tile(gft, e_at + r)
                keep, back_keep = tile(k1, e), tile(k1, r + 1)
                fwd = tuple((keep * d) * s + mixed for d, s in zip(decay, fwd))
                bwd = tuple((back_keep * d) * s + grad for d, s in zip(decay, bwd))
                put(ft, e_at + e, total_of([w * s for w, s in zip(weight, fwd)]))
                put(mx, e_at + r, total_of([w * s for w, s in zip(weight, bwd)]))
            return fwd, bwd

        zero = tuple(jnp.zeros((GROUP, LANES), F32) for _ in range(POLES))
        lax.fori_loop(0, ES // 5, both, (zero, zero))

        @pl.when(c < 2)
        def _():
            along_row(c + 2)

        @pl.when((c == 1) | (c == 2))
        def _():
            entering(c - 1)

        return 0

    lax.fori_loop(0, PARTS - 1, own_filters, 0)
    entering(2)

    def out_copies(c, half):
        rows = pl.ds(pl.multiple_of(half * HALF, HALF), HALF)
        cols = pl.ds(pl.multiple_of(c * WIDTH, WIDTH), WIDTH)
        part_rows = pl.ds(pl.multiple_of(c * GROUP, GROUP), GROUP)
        scale_rows = pl.ds(pl.multiple_of((half * PARTS + c) * GROUP, GROUP), GROUP)
        return [
            pltpu.make_async_remote_copy(
                src_ref=source,
                dst_ref=target,
                send_sem=out_send.at[n, c * 2 + half],
                recv_sem=out_recv.at[n, c * 2 + half],
                device_id={"segment": sg_to},
                device_id_type=MESH,
            )
            for n, (source, target) in enumerate((
                (qv.at[c, rows, :], out_q.at[rows, cols]),
                (sv.at[scale_rows, :], (out_early, out_late)[half].at[part_rows, :]),
            ))
        ]

    def second_pass(c, _):
        @pl.when(c == PARTS - 2)
        def _():
            own_filters(PARTS - 1, 0)

        for k in range(1, PARTS):
            inc_copy(c, k).wait_recv()

        e_at = c * ES
        decay = [tile(dec, c * POLES + p) for p in range(POLES)]
        growth = [tile(grow, c * POLES + p) for p in range(POLES)]
        tap = [tap_t[n, pl.ds(pl.multiple_of(c * GROUP, GROUP), GROUP), :] for n in range(9)]

        def back_step(e, carry):
            fwd, bwd, t1, t2, t22 = carry
            key, value = tile(kt, e_at + e), tile(vt, e_at + e)
            filtered = tile(ft, e_at + e) + tile(mi, e) * total_of(fwd)
            mixed = tile(mx, e_at + e) + tile(mo, e) * total_of(bwd)
            grads = (gtile(c, e) * filtered, mixed * value, mixed * key)
            terms = [
                tap[lag] * grads[0] + tap[3 + lag] * grads[1] + tap[6 + lag] * grads[2]
                for lag in range(3)
            ]
            result = terms[0] + tile(k1, e + 1) * t1 + tile(k2, e + 2) * t22
            fwd = tuple(s * d for s, d in zip(fwd, growth))
            bwd = tuple(s * d for s, d in zip(bwd, decay))
            return result, (fwd, bwd, terms[1], terms[2], t2)

        nothing = jnp.zeros((GROUP, LANES), F32)
        fwd, bwd = [], []
        for p in range(POLES):
            weight = tile(wts, c * POLES + p)
            fwd.append(
                weight * tile(past, c * POLES + p) * tile(inc, cell(c, p // PAIR, 0, p % PAIR))
            )
            bwd.append(weight * decay[p] * tile(inc, cell(c, p // PAIR, 1, p % PAIR)))
        carry = (tuple(fwd), tuple(bwd), nothing, nothing, nothing)
        for e in (TOK + 1, TOK):
            _, carry = back_step(e, carry)

        def piece(n, carry):
            half = 1 - n
            last = half * HALF + HALF - 1

            def backward(i, inner):
                carry, most = inner
                for u in range(4):
                    e = last - (i * 4 + u)
                    result, carry = back_step(e, carry)
                    put(ot, e, result)
                    most = jnp.maximum(most, jnp.abs(result))
                return carry, most

            carry, most = lax.fori_loop(0, HALF // 4, backward, (carry, nothing))
            most = jnp.maximum(most, 1e-30)
            put(sv, half * PARTS + c, most * (1.0 / TOP))
            iv[...] = TOP / most

            def coded(i, _):
                t = half * (HALF // 16) + i
                for g in range(GROUP):
                    value = ot[pl.ds(t * 16 * GROUP + g, 16, stride=GROUP), :] * iv[g : g + 1, :]
                    qv[c, pl.ds(pl.multiple_of(t * 16, 16), 16), g * LANES : (g + 1) * LANES] = (
                        jnp.round(value).astype(jnp.int32).astype(jnp.int16)
                    )
                return 0

            lax.fori_loop(0, HALF // 16, coded, 0)
            for copy in out_copies(c, half):
                copy.start()
            return carry

        for n in range(2):
            carry = piece(n, carry)

        @pl.when(c == 0)
        def _():
            entering(PARTS - 1)

        return 0

    lax.fori_loop(0, PARTS, second_pass, 0)

    def finish(c, _):
        for k in range(1, PARTS):
            tail_copy(c, k).wait_send()
            inc_copy(c, k).wait_send()
        for k in range(1, REACH + 1):
            for way in range(2):
                col_copy(c, way, k).wait_send()
        for half in range(2):
            for copy in out_copies(c, half):
                copy.wait()
        return 0

    for copy in halo_copies:
        copy.wait_send()
    lax.fori_loop(0, PARTS, finish, 0)


def shards(features, cotangent, short_taps, residue, decay_rates, lengths):
    tokens, channels = features.shape[1:]
    far = pl.BlockSpec(memory_space=pltpu.HBM)
    bf16 = jnp.bfloat16
    vm = pltpu.VMEM
    dma = pltpu.SemaphoreType.DMA
    whole = lambda rows: vm((rows * GROUP, LANES), F32)
    coded, late, early = pl.pallas_call(
        mixer_kernel,
        out_shape=(
            jax.ShapeDtypeStruct((tokens, channels), jnp.int16),
            jax.ShapeDtypeStruct((PARTS * GROUP, LANES), F32),
            jax.ShapeDtypeStruct((PARTS * GROUP, LANES), F32),
        ),
        in_specs=[far] * 5 + [pl.BlockSpec(memory_space=pltpu.SMEM)],
        out_specs=(far, far, far),
        scratch_shapes=[
            vm((PARTS, TOK, WIDTH), bf16), vm((PARTS, TOK, WIDTH), bf16),
            vm((2, 16, channels), bf16), vm((16, channels), bf16),
            vm((POLES, channels), F32), vm((POLES, channels), F32),
            vm((PARTS, XS * GROUP, LANES), F32), vm((PARTS, ES * GROUP, LANES), F32),
            whole(PARTS * ES), whole(PARTS * ES), whole(PARTS * ES), whole(PARTS * ES),
            whole(PARTS * ES), whole(ES), whole(XS), whole(XS), whole(XS), whole(XS),
            whole(XS), whole(XS),
            vm((9, PARTS * GROUP, LANES), F32), whole(PARTS * POLES), whole(PARTS * POLES),
            whole(PARTS * POLES), whole(PARTS * POLES),
            whole(PARTS * POLES), whole(PARTS * POLES), whole(PARTS * POLES),
            whole(PARTS * 2 * POLES), whole(PARTS * 2 * POLES), whole(PARTS * CELL),
            whole(PARTS * REACH * CELL), whole(PARTS * 2 * POLES), whole(PARTS * 2 * POLES),
            whole(2 * PARTS), whole(2 * PARTS),
            vm((PARTS, TOK, WIDTH), jnp.int16), whole(2 * PARTS), whole(1),
            dma((2, PARTS)), dma((3,)), dma((3,)), dma((3,)),
            dma((PARTS, PARTS)), dma((PARTS, PARTS)),
            dma((PARTS, 2 * REACH)), dma((PARTS, 2 * REACH)),
            dma((PARTS, PARTS)), dma((PARTS, PARTS)), dma((2, 2 * PARTS)), dma((2, 2 * PARTS)),
            dma((3,)),
        ],
        compiler_params=pltpu.CompilerParams(
            collective_id=0, has_side_effects=True, vmem_limit_bytes=60 * 1024 * 1024
        ),
        cost_estimate=pl.CostEstimate(
            flops=160 * tokens * channels, bytes_accessed=8 * tokens * channels, transcendentals=0
        ),
    )(features, cotangent, short_taps.reshape(9, channels // LANES, LANES), residue, decay_rates, lengths)
    first_half = (jnp.arange(tokens) < HALF)[:, None]
    scale = jnp.where(first_half, early.reshape(1, channels), late.reshape(1, channels))
    return (coded.astype(F32) * scale)[None]


def solution(mesh):
    in_specs = (
        P("segment", "seq", None),
        P("segment", "seq", None),
        P("segment", None, None, None),
        P("segment", None, None),
        P("segment", None, None),
        P("segment", None),
    )
    out_specs = P("segment", "seq", None)
    return jax.shard_map(shards, mesh=mesh, in_specs=in_specs, out_specs=out_specs, check_vma=False)
```

```python
import jax
import jax.numpy as jnp
from jax import lax
from jax.experimental import pallas as pl
from jax.experimental.pallas import tpu as pltpu
from jax.sharding import PartitionSpec as P

MESH = pl.DeviceIdType.MESH
F32 = jnp.float32
TOK = 128
HALO = 2
LANES = 128
GROUP = 8
WIDTH = GROUP * LANES
PARTS = 4
POLES = 8
DOCS = 8
ROWS = 8
REACH = 4
XS = TOK + 2 * HALO
ES = TOK + HALO
HALF = TOK // 2
STATE = POLES * GROUP
PAIR = POLES // PARTS
CELL = 2 * PAIR
TOP = 32767.0
LENT = PARTS - 1
OWN = LENT * WIDTH


def tile(ref, i):
    return ref[pl.ds(pl.multiple_of(i * GROUP, GROUP), GROUP), :]


def put(ref, i, value):
    ref[pl.ds(pl.multiple_of(i * GROUP, GROUP), GROUP), :] = value


def total_of(values):
    values = list(values)
    while len(values) > 1:
        values = [a + b for a, b in zip(values[::2], values[1::2])] + (
            [values[-1]] if len(values) % 2 else []
        )
    return values[0]


def mixer_kernel(
    feat, cot, taps, res, rates, lens, out_q, out_late, out_early,
    feat_v, cot_v, feat_e, cot_e, rim_lent, res_v, rates_v,
    xt, gt, kt, vt, gft, ft, mx, ot, k1, k2, mt, mh, mi, mo,
    tap_t, dec, wts, near, past, grow, dd, dd4,
    tails, row_in, sums, col_in, sent, inc, row_link, col_link, ends_own, ends_lent, qv, sv, iv,
    load_sem, par_sem, halo_send, halo_recv, tail_send, tail_recv,
    col_send, col_recv, inc_send, inc_recv, out_send, out_recv, rim_sem, lend_send, lend_recv, kept_sem, ready,
):
    sg = lax.axis_index("segment")
    q = lax.axis_index("seq")
    n_sg = lax.axis_size("segment")
    n_q = lax.axis_size("seq")
    y, x = q // PARTS, q % PARTS
    before, after = (q + n_q - 1) % n_q, (q + 1) % n_q
    sg_to, sg_from = (sg + n_sg - 1) % n_sg, (sg + 1) % n_sg

    def row_mate(k):
        return y * PARTS + (x + k) % PARTS

    def col_mate(k):
        return ((y + k) % ROWS) * PARTS + x

    loads = []
    for c in range(LENT):
        cols = pl.ds(c * WIDTH, WIDTH)
        loads.append((
            pltpu.make_async_copy(feat.at[0, :, cols], feat_v.at[c], load_sem.at[0, c]),
            pltpu.make_async_copy(cot.at[0, :, cols], cot_v.at[c], load_sem.at[1, c]),
        ))
    pars = [
        pltpu.make_async_copy(
            taps.at[:, pl.ds(0, LENT * GROUP), :],
            tap_t.at[:, pl.ds(0, LENT * GROUP), :],
            par_sem.at[0],
        ),
        pltpu.make_async_copy(
            res.at[0, :, pl.ds(0, OWN)], res_v.at[:, pl.ds(0, OWN)], par_sem.at[1]
        ),
        pltpu.make_async_copy(
            rates.at[0, :, pl.ds(0, OWN)], rates_v.at[:, pl.ds(0, OWN)], par_sem.at[2]
        ),
    ]
    rim = [
        pltpu.make_async_copy(feat.at[0, pl.ds(0, 16), :], feat_e.at[0], rim_sem.at[0]),
        pltpu.make_async_copy(feat.at[0, pl.ds(TOK - 16, 16), :], feat_e.at[1], rim_sem.at[1]),
        pltpu.make_async_copy(cot.at[0, pl.ds(0, 16), :], cot_e, rim_sem.at[2]),
    ]
    for copy in rim:
        copy.start()
    for copy in loads[0]:
        copy.start()
    for copy in pars:
        copy.start()
    for pair in loads[1:]:
        for copy in pair:
            copy.start()

    barrier = pltpu.get_barrier_semaphore()

    def greet(**where):
        pl.semaphore_signal(barrier, inc=1, device_id=where, device_id_type=MESH)

    for k in range(1, PARTS):
        greet(seq=row_mate(k))
    for k in range(1, ROWS):
        greet(seq=col_mate(k))
    greet(seq=before)
    greet(seq=after)
    last_sg = n_sg - 1
    three = (q, before, after)

    @pl.when(sg != last_sg)
    def _():
        for near_q in three:
            greet(segment=sg_from, seq=near_q)

    @pl.when(sg == 0)
    def _():
        for near_q in three:
            greet(segment=sg_to, seq=near_q)


    run = jnp.int32(0)
    for i in range(DOCS):
        run = run + lens[0, i]
        ends_own[i * GROUP : (i + 1) * GROUP, :] = jnp.full((GROUP, LANES), run, jnp.int32)

    def doc_finder(ends_ref):
        ends = [ends_ref[i * GROUP : (i + 1) * GROUP, :] for i in range(DOCS)]

        def doc_at(position):
            spot = jnp.full((GROUP, LANES), position, jnp.int32)
            count = total_of([jnp.where(end <= spot, 1, 0) for end in ends])
            return jnp.where(spot < 0, -1, count)

        return doc_at

    def same(a, b):
        return jnp.where(a == b, 1.0, 0.0).astype(F32)

    first = q * TOK
    row_first = y * PARTS * TOK
    row_span = TOK * PARTS

    def masks(ends_ref, which):
        doc_at = doc_finder(ends_ref)
        doc_tail = doc_at(first + TOK - 1)
        doc_head = doc_at(first + HALO)
        doc_in = doc_at(first - 1)
        doc_out = doc_at(first + ES)
        at = which * XS

        def mask_step(e, carry):
            d1, d2 = carry
            d0 = doc_at(first + e)
            put(k1, at + e, same(d0, d1))
            put(k2, at + e, same(d0, d2))
            put(mt, at + e, same(d0, doc_tail))
            put(mh, at + e, same(d0, doc_head))
            put(mi, at + e, same(d0, doc_in))
            put(mo, at + e, same(d0, doc_out))
            return d0, d1

        lax.fori_loop(0, XS, mask_step, (doc_at(first - 1), doc_at(first - 2)))

        fwd = [doc_at(row_first + n * TOK - 1) for n in range(PARTS + 1)]
        bwd = [doc_at(row_first + n * TOK + HALO) for n in range(PARTS + 1)]
        gone = [doc_at(row_first - k * row_span - 1) for k in range(REACH)]
        coming = [doc_at(row_first + k * row_span + HALO) for k in range(1, REACH + 1)]
        for ref, pairs in ((row_link, (fwd, bwd)), (col_link, (gone, coming))):
            for way, docs in enumerate(pairs):
                for n in range(len(docs) - 1):
                    put(ref, (which * 2 + way) * PARTS + n, same(docs[n], docs[n + 1]))

    masks(ends_own, 0)

    def move(source, target, shift, c, t):
        for g in range(GROUP):
            value = source[
                c, pl.ds(pl.multiple_of(t * 16, 16), 16), g * LANES : (g + 1) * LANES
            ].astype(F32)
            target[c, pl.ds((shift + t * 16) * GROUP + g, 16, stride=GROUP), :] = value

    def relay(c, lent):
        if not lent:
            for which, (far, near_v) in enumerate(((feat, feat_v), (cot, cot_v))):
                pltpu.make_async_copy(
                    far.at[0, :, pl.ds(0, WIDTH)], near_v.at[c], load_sem.at[which, c]
                ).wait()

        def rows(t, _):
            move(feat_v, xt, HALO, c, t)
            move(cot_v, gt, 0, c, t)
            return 0

        tiles = TOK // 16
        if lent:
            lax.fori_loop(0, tiles, rows, 0)
            for n, (target, slot, row) in enumerate((
                (xt, 0, 16 - HALO), (xt, TOK + HALO, 0), (gt, TOK, 0)
            )):
                for g in range(GROUP):
                    value = rim_lent[n, :, g * LANES : (g + 1) * LANES].astype(F32)
                    target[c, pl.ds(slot * GROUP + g, HALO, stride=GROUP), :] = value[
                        row : row + HALO
                    ]
        else:
            lax.fori_loop(1, tiles - 1, rows, 0)
            move(cot_v, gt, 0, c, tiles - 1)

    def halo_set(parts, at):
        return [
            pltpu.make_async_remote_copy(
                src_ref=ref.at[parts, pl.ds(here * GROUP, HALO * GROUP), :],
                dst_ref=ref.at[parts, pl.ds(there * GROUP, HALO * GROUP), :],
                send_sem=halo_send.at[at + n],
                recv_sem=halo_recv.at[at + n],
                device_id={"seq": to},
                device_id_type=MESH,
            )
            for n, (ref, here, there, to) in enumerate((
                (xt, TOK, 0, after),
                (xt, HALO, TOK + HALO, before),
                (gt, 0, TOK, before),
            ))
        ]

    halo_copies = halo_set(pl.ds(0, LENT), 0)

    lent_cols = pl.ds(OWN, WIDTH)
    lent_tiles = pl.ds(LENT * GROUP, GROUP)
    lend_copies = [
        pltpu.make_async_remote_copy(
            src_ref=source,
            dst_ref=target,
            send_sem=lend_send.at[n],
            recv_sem=lend_recv.at[n],
            device_id={"segment": sg_to, "seq": to},
            device_id_type=MESH,
        )
        for n, (source, target, to) in enumerate((
            (ends_own, ends_lent, q),
            (taps.at[:, lent_tiles, :], tap_t.at[:, lent_tiles, :], q),
            (res.at[0, :, lent_cols], res_v.at[:, lent_cols], q),
            (rates.at[0, :, lent_cols], rates_v.at[:, lent_cols], q),
            (feat.at[0, pl.ds(TOK - 16, 16), lent_cols], rim_lent.at[0], after),
            (feat.at[0, pl.ds(0, 16), lent_cols], rim_lent.at[1], before),
            (cot.at[0, pl.ds(0, 16), lent_cols], rim_lent.at[2], before),
            (feat.at[0, :, lent_cols], feat_v.at[LENT], q),
            (cot.at[0, :, lent_cols], cot_v.at[LENT], q),
        ))
    ]

    for copy in rim:
        copy.wait()
    for c in range(LENT):
        for g in range(GROUP):
            cols = slice(c * WIDTH + g * LANES, c * WIDTH + (g + 1) * LANES)
            spread = pl.ds(HALO * GROUP + g, 16, stride=GROUP)
            xt[c, spread, :] = feat_e[0, :, cols].astype(F32)
            spread = pl.ds((HALO + TOK - 16) * GROUP + g, 16, stride=GROUP)
            xt[c, spread, :] = feat_e[1, :, cols].astype(F32)
            gt[c, pl.ds(g, 16, stride=GROUP), :] = cot_e[:, cols].astype(F32)
    across = len(three) * ((sg + last_sg) // n_sg + sg // last_sg)
    pl.semaphore_wait(barrier, (PARTS - 1) + (ROWS - 1) + 2 + across)
    for copy in halo_copies:
        copy.start()

    @pl.when(sg == last_sg)
    def _():
        for near_q in three:
            pl.semaphore_signal(
                ready, inc=1, device_id={"segment": sg_from, "seq": near_q}, device_id_type=MESH
            )

    @pl.when(sg != 0)
    def _():
        for copy in lend_copies:
            copy.start()


    def parameters(c):
        for g in range(GROUP):
            cols = slice(c * WIDTH + g * LANES, c * WIDTH + (g + 1) * LANES)
            rate = rates_v[:, cols]
            spread = pl.ds(c * STATE + g, POLES, stride=GROUP)
            dec[spread, :] = jnp.exp(-rate)
            near[spread, :] = jnp.exp(-rate * float(TOK - HALO))
            past[spread, :] = jnp.exp(-rate * float(ES))
            grow[spread, :] = jnp.exp(rate)
            dd[spread, :] = jnp.exp(-rate * float(TOK))
            dd4[spread, :] = jnp.exp(-rate * float(TOK * PARTS))
            wts[spread, :] = res_v[:, cols] * jnp.sqrt(2.0 * rate)

    for copy in pars:
        copy.wait()
    for c in range(LENT):
        parameters(c)

    def cells(ref, at, count=CELL):
        return ref.at[pl.ds(pl.multiple_of(at * GROUP, GROUP), count * GROUP), :]

    def cell(c, who, way, pole):
        return ((c * PARTS + who) * 2 + way) * PAIR + pole

    def tail_copy(c, k):
        other = (x + k) % PARTS
        return pltpu.make_async_remote_copy(
            src_ref=cells(tails, cell(c, other, 0, 0)),
            dst_ref=cells(row_in, cell(c, x, 0, 0)),
            send_sem=tail_send.at[c, k],
            recv_sem=tail_recv.at[c, k],
            device_id={"seq": row_mate(k)},
            device_id_type=MESH,
        )

    def col_copy(c, way, k):
        slot = way * REACH + k - 1
        return pltpu.make_async_remote_copy(
            src_ref=cells(sums, (c * 2 + way) * PAIR, PAIR),
            dst_ref=cells(col_in, (c * 2 * REACH + slot) * PAIR, PAIR),
            send_sem=col_send.at[c, slot],
            recv_sem=col_recv.at[c, slot],
            device_id={"seq": col_mate(k if way == 0 else ROWS - k)},
            device_id_type=MESH,
        )

    def inc_copy(c, k):
        other = (x + k) % PARTS
        return pltpu.make_async_remote_copy(
            src_ref=cells(sent, cell(c, other, 0, 0)),
            dst_ref=cells(inc, cell(c, x, 0, 0)),
            send_sem=inc_send.at[c, k],
            recv_sem=inc_recv.at[c, k],
            device_id={"seq": row_mate(k)},
            device_id_type=MESH,
        )

    def along_row(c):
        for k in range(1, PARTS):
            tail_copy(c, k).wait_recv()
        for pole in range(PAIR):
            span = tile(dd, c * POLES + x * PAIR + pole)
            for way in range(2):
                order = list(range(PARTS)) if way == 0 else list(range(PARTS - 1, -1, -1))
                state = tile(row_in, cell(c, order[0], way, pole))
                for n in order[1:]:
                    link = tile(row_link, ((c // LENT) * 2 + way) * PARTS + n)
                    state = tile(row_in, cell(c, n, way, pole)) + link * span * state
                put(sums, (c * 2 + way) * PAIR + pole, state)
        for k in range(1, REACH + 1):
            for way in range(2):
                col_copy(c, way, k).start()

    def entering(c):
        for k in range(1, REACH + 1):
            for way in range(2):
                col_copy(c, way, k).wait_recv()
        for pole in range(PAIR):
            at = c * POLES + x * PAIR + pole
            span, long_span = tile(dd, at), tile(dd4, at)
            for way in range(2):
                slot = (c * 2 + way) * REACH
                state = tile(col_in, (slot + REACH - 1) * PAIR + pole)
                for k in range(REACH - 1, 0, -1):
                    link = tile(col_link, ((c // LENT) * 2 + way) * PARTS + k - 1)
                    state = tile(col_in, (slot + k - 1) * PAIR + pole) + link * long_span * state
                order = range(PARTS) if way == 0 else range(PARTS - 1, -1, -1)
                for n in order:
                    put(sent, cell(c, n, way, pole), state)
                    link = tile(row_link, ((c // LENT) * 2 + way) * PARTS + n)
                    state = tile(row_in, cell(c, n, way, pole)) + link * span * state
        for k in range(1, PARTS):
            inc_copy(c, k).start()
        for n in range(CELL):
            put(inc, cell(c, x, 0, n), tile(sent, cell(c, x, 0, n)))

    def xtile(c, slot):
        return xt[c, pl.ds(pl.multiple_of(slot * GROUP, GROUP), GROUP), :]

    def gtile(c, e):
        return gt[c, pl.ds(pl.multiple_of(e * GROUP, GROUP), GROUP), :]

    def first_pass(c, lent):
        relay(c, lent)
        m_at = (c // LENT) * XS
        tap = [tap_t[n, pl.ds(pl.multiple_of(c * GROUP, GROUP), GROUP), :] for n in range(9)]
        e_at = c * ES

        def stream(e, x1, x2):
            x0 = xtile(c, HALO + e)
            a, b = x1 * tile(k1, m_at + e), x2 * tile(k2, m_at + e)
            gate, key, value = (
                tap[3 * n] * x0 + tap[3 * n + 1] * a + tap[3 * n + 2] * b for n in range(3)
            )
            grad = gtile(c, e) * gate
            put(kt, e_at + e, key)
            put(vt, e_at + e, value)
            put(gft, e_at + e, grad)
            return x0, key * value, grad

        def streams(i, carry):
            x1, x2 = carry
            for u in range(6):
                x0, _, _ = stream(HALO + i * 6 + u, x1, x2)
                x1, x2 = x0, x1
            return x1, x2

        inner = TOK - HALO
        lax.fori_loop(0, inner // 6, streams, (xtile(c, HALO + 1), xtile(c, HALO)))

        decay = [tile(dec, c * POLES + p) for p in range(POLES)]

        def ends_step(i, carry):
            fwd, bwd = carry
            for u in range(3):
                e = HALO + i * 3 + u
                r = TOK - 1 - (i * 3 + u)
                mixed = tile(kt, e_at + e) * tile(vt, e_at + e) * tile(mt, m_at + e)
                grad = tile(gft, e_at + r) * tile(mh, m_at + r)
                fwd = tuple(d * s + mixed for d, s in zip(decay, fwd))
                bwd = tuple(d * s + grad for d, s in zip(decay, bwd))
            return fwd, bwd

        zero = tuple(jnp.zeros((GROUP, LANES), F32) for _ in range(POLES))
        fwd, bwd = lax.fori_loop(0, inner // 3, ends_step, (zero, zero))

        if not lent:

            @pl.when(c == 0)
            def _():
                for copy in halo_copies:
                    copy.wait_recv()

        x0, mixed0, _ = stream(0, xtile(c, 1), xtile(c, 0))
        _, mixed1, _ = stream(1, x0, xtile(c, 1))
        x0, _, grad0 = stream(TOK, xtile(c, TOK + 1), xtile(c, TOK))
        _, _, grad1 = stream(TOK + 1, x0, xtile(c, TOK + 1))
        mixed0, mixed1 = mixed0 * tile(mt, m_at), mixed1 * tile(mt, m_at + 1)
        grad0 = grad0 * tile(mh, m_at + TOK)
        grad1 = grad1 * tile(mh, m_at + TOK + 1)
        for p in range(POLES):
            far = tile(near, c * POLES + p)
            at = (c, p // PAIR)
            put(tails, cell(*at, 0, p % PAIR), fwd[p] + far * (decay[p] * mixed0 + mixed1))
            put(tails, cell(*at, 1, p % PAIR), bwd[p] + far * (decay[p] * grad1 + grad0))
        for k in range(1, PARTS):
            tail_copy(c, k).start()
        for n in range(CELL):
            put(row_in, cell(c, x, 0, n), tile(tails, cell(c, x, 0, n)))

        return 0

    def own_filters(c):
        e_at = c * ES
        m_at = (c // LENT) * XS
        decay = [tile(dec, c * POLES + p) for p in range(POLES)]
        weight = [tile(wts, c * POLES + p) for p in range(POLES)]

        def both(i, carry):
            fwd, bwd = carry
            for u in range(5):
                e = i * 5 + u
                r = ES - 1 - e
                mixed = tile(kt, e_at + e) * tile(vt, e_at + e)
                grad = tile(gft, e_at + r)
                keep, back_keep = tile(k1, m_at + e), tile(k1, m_at + r + 1)
                fwd = tuple((keep * d) * s + mixed for d, s in zip(decay, fwd))
                bwd = tuple((back_keep * d) * s + grad for d, s in zip(decay, bwd))
                put(ft, e_at + e, total_of([w * s for w, s in zip(weight, fwd)]))
                put(mx, e_at + r, total_of([w * s for w, s in zip(weight, bwd)]))
            return fwd, bwd

        zero = tuple(jnp.zeros((GROUP, LANES), F32) for _ in range(POLES))
        lax.fori_loop(0, ES // 5, both, (zero, zero))

    lax.fori_loop(0, LENT, lambda c, _: first_pass(c, False), 0)
    for copy in lend_copies[:4]:
        copy.wait_recv()
    masks(ends_lent, 1)
    parameters(LENT)
    along_row(0)

    @pl.when(sg == 0)
    def _():
        pl.semaphore_wait(ready, len(three))
        for copy in lend_copies:
            copy.start()

    for copy in lend_copies[4:]:
        copy.wait_recv()
    first_pass(LENT, True)
    along_row(1)
    own_filters(0)
    along_row(2)
    own_filters(1)
    entering(0)
    along_row(LENT)
    own_filters(2)
    entering(1)

    def out_copies(c, half):
        rows = pl.ds(pl.multiple_of(half * HALF, HALF), HALF)
        cols = pl.ds(pl.multiple_of(c * WIDTH, WIDTH), WIDTH)
        part_rows = pl.ds(pl.multiple_of(c * GROUP, GROUP), GROUP)
        scale_rows = pl.ds(pl.multiple_of((half * PARTS + c) * GROUP, GROUP), GROUP)
        return [
            pltpu.make_async_remote_copy(
                src_ref=source,
                dst_ref=target,
                send_sem=out_send.at[n, c * 2 + half],
                recv_sem=out_recv.at[n, c * 2 + half],
                device_id={"segment": sg_to},
                device_id_type=MESH,
            )
            for n, (source, target) in enumerate((
                (qv.at[c, rows, :], out_q.at[rows, cols]),
                (sv.at[scale_rows, :], (out_early, out_late)[half].at[part_rows, :]),
            ))
        ]

    def kept_copies(half):
        rows = pl.ds(half * HALF, HALF)
        scale_rows = pl.ds((half * PARTS + LENT) * GROUP, GROUP)
        return [
            pltpu.make_async_copy(
                qv.at[LENT, rows, :], out_q.at[rows, lent_cols], kept_sem.at[0, half]
            ),
            pltpu.make_async_copy(
                sv.at[scale_rows, :],
                (out_early, out_late)[half].at[lent_tiles, :],
                kept_sem.at[1, half],
            ),
        ]

    def second_pass(c, _):
        for k in range(1, PARTS):
            inc_copy(c, k).wait_recv()

        e_at = c * ES
        m_at = (c // LENT) * XS
        decay = [tile(dec, c * POLES + p) for p in range(POLES)]
        growth = [tile(grow, c * POLES + p) for p in range(POLES)]
        tap = [tap_t[n, pl.ds(pl.multiple_of(c * GROUP, GROUP), GROUP), :] for n in range(9)]

        def back_step(e, carry):
            fwd, bwd, t1, t2, t22 = carry
            key, value = tile(kt, e_at + e), tile(vt, e_at + e)
            filtered = tile(ft, e_at + e) + tile(mi, m_at + e) * total_of(fwd)
            mixed = tile(mx, e_at + e) + tile(mo, m_at + e) * total_of(bwd)
            grads = (gtile(c, e) * filtered, mixed * value, mixed * key)
            terms = [
                tap[lag] * grads[0] + tap[3 + lag] * grads[1] + tap[6 + lag] * grads[2]
                for lag in range(3)
            ]
            result = terms[0] + tile(k1, m_at + e + 1) * t1 + tile(k2, m_at + e + 2) * t22
            fwd = tuple(s * d for s, d in zip(fwd, growth))
            bwd = tuple(s * d for s, d in zip(bwd, decay))
            return result, (fwd, bwd, terms[1], terms[2], t2)

        nothing = jnp.zeros((GROUP, LANES), F32)
        fwd, bwd = [], []
        for p in range(POLES):
            weight = tile(wts, c * POLES + p)
            fwd.append(
                weight * tile(past, c * POLES + p) * tile(inc, cell(c, p // PAIR, 0, p % PAIR))
            )
            bwd.append(weight * decay[p] * tile(inc, cell(c, p // PAIR, 1, p % PAIR)))
        carry = (tuple(fwd), tuple(bwd), nothing, nothing, nothing)
        for e in (TOK + 1, TOK):
            _, carry = back_step(e, carry)

        def piece(n, carry):
            half = 1 - n
            last = half * HALF + HALF - 1

            def backward(i, inner):
                carry, most = inner
                for u in range(4):
                    e = last - (i * 4 + u)
                    result, carry = back_step(e, carry)
                    put(ot, e, result)
                    most = jnp.maximum(most, jnp.abs(result))
                return carry, most

            carry, most = lax.fori_loop(0, HALF // 4, backward, (carry, nothing))
            most = jnp.maximum(most, 1e-30)
            put(sv, half * PARTS + c, most * (1.0 / TOP))
            iv[...] = TOP / most

            def coded(i, _):
                t = half * (HALF // 16) + i
                for g in range(GROUP):
                    value = ot[pl.ds(t * 16 * GROUP + g, 16, stride=GROUP), :] * iv[g : g + 1, :]
                    qv[c, pl.ds(pl.multiple_of(t * 16, 16), 16), g * LANES : (g + 1) * LANES] = (
                        jnp.round(value).astype(jnp.int32).astype(jnp.int16)
                    )
                return 0

            lax.fori_loop(0, HALF // 16, coded, 0)

            @pl.when(c < LENT)
            def _():
                for copy in out_copies(c, half):
                    copy.start()

            @pl.when(c == LENT)
            def _():
                for copy in kept_copies(half):
                    copy.start()

            return carry

        for n in range(2):
            carry = piece(n, carry)

        @pl.when(c == 0)
        def _():
            entering(2)

        @pl.when(c == 1)
        def _():
            entering(LENT)
            own_filters(LENT)

        return 0

    lax.fori_loop(0, PARTS, second_pass, 0)

    def finish(c, _):
        for k in range(1, PARTS):
            tail_copy(c, k).wait_send()
            inc_copy(c, k).wait_send()
        for k in range(1, REACH + 1):
            for way in range(2):
                col_copy(c, way, k).wait_send()
        return 0

    def finish_out(c, _):
        for half in range(2):
            for copy in out_copies(c, half):
                copy.wait()
        return 0

    for copy in halo_copies + lend_copies:
        copy.wait_send()
    lax.fori_loop(0, PARTS, finish, 0)
    lax.fori_loop(0, LENT, finish_out, 0)
    for half in range(2):
        for copy in kept_copies(half):
            copy.wait()


def shards(features, cotangent, short_taps, residue, decay_rates, lengths):
    tokens, channels = features.shape[1:]
    far = pl.BlockSpec(memory_space=pltpu.HBM)
    bf16 = jnp.bfloat16
    vm = pltpu.VMEM
    dma = pltpu.SemaphoreType.DMA
    whole = lambda rows: vm((rows * GROUP, LANES), F32)
    coded, late, early = pl.pallas_call(
        mixer_kernel,
        out_shape=(
            jax.ShapeDtypeStruct((tokens, channels), jnp.int16),
            jax.ShapeDtypeStruct((PARTS * GROUP, LANES), F32),
            jax.ShapeDtypeStruct((PARTS * GROUP, LANES), F32),
        ),
        in_specs=[far] * 5 + [pl.BlockSpec(memory_space=pltpu.SMEM)],
        out_specs=(far, far, far),
        scratch_shapes=[
            vm((PARTS, TOK, WIDTH), bf16), vm((PARTS, TOK, WIDTH), bf16),
            vm((2, 16, channels), bf16), vm((16, channels), bf16), vm((3, 16, WIDTH), bf16),
            vm((POLES, channels), F32), vm((POLES, channels), F32),
            vm((PARTS, XS * GROUP, LANES), F32), vm((PARTS, ES * GROUP, LANES), F32),
            whole(PARTS * ES), whole(PARTS * ES), whole(PARTS * ES), whole(PARTS * ES),
            whole(PARTS * ES), whole(ES), whole(2 * XS), whole(2 * XS), whole(2 * XS),
            whole(2 * XS), whole(2 * XS), whole(2 * XS),
            vm((9, PARTS * GROUP, LANES), F32), whole(PARTS * POLES), whole(PARTS * POLES),
            whole(PARTS * POLES), whole(PARTS * POLES),
            whole(PARTS * POLES), whole(PARTS * POLES), whole(PARTS * POLES),
            whole(PARTS * 2 * POLES), whole(PARTS * 2 * POLES), whole(PARTS * CELL),
            whole(PARTS * REACH * CELL), whole(PARTS * 2 * POLES), whole(PARTS * 2 * POLES),
            whole(4 * PARTS), whole(4 * PARTS),
            vm((DOCS * GROUP, LANES), jnp.int32), vm((DOCS * GROUP, LANES), jnp.int32),
            vm((PARTS, TOK, WIDTH), jnp.int16), whole(2 * PARTS), whole(1),
            dma((2, PARTS)), dma((3,)), dma((3,)), dma((3,)),
            dma((PARTS, PARTS)), dma((PARTS, PARTS)),
            dma((PARTS, 2 * REACH)), dma((PARTS, 2 * REACH)),
            dma((PARTS, PARTS)), dma((PARTS, PARTS)), dma((2, 2 * PARTS)), dma((2, 2 * PARTS)),
            dma((3,)), dma((9,)), dma((9,)), dma((2, 2)),
            pltpu.SemaphoreType.REGULAR,
        ],
        compiler_params=pltpu.CompilerParams(
            collective_id=0, has_side_effects=True, vmem_limit_bytes=60 * 1024 * 1024
        ),
        cost_estimate=pl.CostEstimate(
            flops=160 * tokens * channels, bytes_accessed=8 * tokens * channels, transcendentals=0
        ),
    )(features, cotangent, short_taps.reshape(9, channels // LANES, LANES), residue, decay_rates, lengths)
    first_half = (jnp.arange(tokens) < HALF)[:, None]
    scale = jnp.where(first_half, early.reshape(1, channels), late.reshape(1, channels))
    return (coded.astype(F32) * scale)[None]


def solution(mesh):
    in_specs = (
        P("segment", "seq", None),
        P("segment", "seq", None),
        P("segment", None, None, None),
        P("segment", None, None),
        P("segment", None, None),
        P("segment", None),
    )
    out_specs = P("segment", "seq", None)
    return jax.shard_map(shards, mesh=mesh, in_specs=in_specs, out_specs=out_specs, check_vma=False)
```

```python
import jax
import jax.numpy as jnp
from jax import lax
from jax.experimental import pallas as pl
from jax.experimental.pallas import tpu as pltpu
from jax.sharding import PartitionSpec as P

MESH = pl.DeviceIdType.MESH
F32 = jnp.float32
TOK = 128
HALO = 2
LANES = 128
GROUP = 8
WIDTH = GROUP * LANES
PARTS = 4
POLES = 8
DOCS = 8
ROWS = 8
REACH = 4
XS = TOK + 2 * HALO
ES = TOK + HALO
HALF = TOK // 2
STATE = POLES * GROUP
PAIR = POLES // PARTS
CELL = 2 * PAIR
TOP = 32767.0
LENT = PARTS - 1
OWN = LENT * WIDTH


def tile(ref, i):
    return ref[pl.ds(pl.multiple_of(i * GROUP, GROUP), GROUP), :]


def put(ref, i, value):
    ref[pl.ds(pl.multiple_of(i * GROUP, GROUP), GROUP), :] = value


def total_of(values):
    values = list(values)
    while len(values) > 1:
        values = [a + b for a, b in zip(values[::2], values[1::2])] + (
            [values[-1]] if len(values) % 2 else []
        )
    return values[0]


def mixer_kernel(
    feat, cot, taps, res, rates, lens, out_q, out_late, out_early,
    feat_v, cot_v, feat_e, cot_e, rim_lent, res_v, rates_v,
    xt, gt, kt, vt, gft, ft, mx, ot, k1, k2, mt, mh, mi, mo,
    tap_t, dec, wts, near, past, grow, dd, dd4,
    tails, row_in, sums, col_in, sent, inc, row_link, col_link, ends_own, ends_lent, qv, sv, iv,
    load_sem, par_sem, halo_send, halo_recv, tail_send, tail_recv,
    col_send, col_recv, inc_send, inc_recv, out_send, out_recv, rim_sem, lend_send, lend_recv, kept_sem, ready,
):
    sg = lax.axis_index("segment")
    q = lax.axis_index("seq")
    n_sg = lax.axis_size("segment")
    n_q = lax.axis_size("seq")
    y, x = q // PARTS, q % PARTS
    before, after = (q + n_q - 1) % n_q, (q + 1) % n_q
    sg_to, sg_from = (sg + n_sg - 1) % n_sg, (sg + 1) % n_sg

    def row_mate(k):
        return y * PARTS + (x + k) % PARTS

    def col_mate(k):
        return ((y + k) % ROWS) * PARTS + x

    barrier = pltpu.get_barrier_semaphore()

    def greet(**where):
        pl.semaphore_signal(barrier, inc=1, device_id=where, device_id_type=MESH)

    for k in range(1, PARTS):
        greet(seq=row_mate(k))
    for k in range(1, ROWS):
        greet(seq=col_mate(k))
    greet(seq=before)
    greet(seq=after)
    last_sg = n_sg - 1
    three = (q, before, after)

    @pl.when(sg != last_sg)
    def _():
        for near_q in three:
            greet(segment=sg_from, seq=near_q)

    @pl.when(sg == 0)
    def _():
        for near_q in three:
            greet(segment=sg_to, seq=near_q)


    loads = []
    for c in range(LENT):
        cols = pl.ds(c * WIDTH, WIDTH)
        loads.append((
            pltpu.make_async_copy(feat.at[0, :, cols], feat_v.at[c], load_sem.at[0, c]),
            pltpu.make_async_copy(cot.at[0, :, cols], cot_v.at[c], load_sem.at[1, c]),
        ))
    pars = [
        pltpu.make_async_copy(
            taps.at[:, pl.ds(0, LENT * GROUP), :],
            tap_t.at[:, pl.ds(0, LENT * GROUP), :],
            par_sem.at[0],
        ),
        pltpu.make_async_copy(
            res.at[0, :, pl.ds(0, OWN)], res_v.at[:, pl.ds(0, OWN)], par_sem.at[1]
        ),
        pltpu.make_async_copy(
            rates.at[0, :, pl.ds(0, OWN)], rates_v.at[:, pl.ds(0, OWN)], par_sem.at[2]
        ),
    ]
    rim = [
        pltpu.make_async_copy(feat.at[0, pl.ds(0, 16), :], feat_e.at[0], rim_sem.at[0]),
        pltpu.make_async_copy(feat.at[0, pl.ds(TOK - 16, 16), :], feat_e.at[1], rim_sem.at[1]),
        pltpu.make_async_copy(cot.at[0, pl.ds(0, 16), :], cot_e, rim_sem.at[2]),
    ]
    for copy in rim:
        copy.start()
    for copy in loads[0]:
        copy.start()
    for copy in pars:
        copy.start()
    for pair in loads[1:]:
        for copy in pair:
            copy.start()

    run = jnp.int32(0)
    for i in range(DOCS):
        run = run + lens[0, i]
        ends_own[i * GROUP : (i + 1) * GROUP, :] = jnp.full((GROUP, LANES), run, jnp.int32)

    def doc_finder(ends_ref):
        ends = [ends_ref[i * GROUP : (i + 1) * GROUP, :] for i in range(DOCS)]

        def doc_at(position):
            spot = jnp.full((GROUP, LANES), position, jnp.int32)
            count = total_of([jnp.where(end <= spot, 1, 0) for end in ends])
            return jnp.where(spot < 0, -1, count)

        return doc_at

    def same(a, b):
        return jnp.where(a == b, 1.0, 0.0).astype(F32)

    first = q * TOK
    row_first = y * PARTS * TOK
    row_span = TOK * PARTS

    def masks(ends_ref, which):
        doc_at = doc_finder(ends_ref)
        doc_tail = doc_at(first + TOK - 1)
        doc_head = doc_at(first + HALO)
        doc_in = doc_at(first - 1)
        doc_out = doc_at(first + ES)
        at = which * XS

        def mask_step(e, carry):
            d1, d2 = carry
            d0 = doc_at(first + e)
            put(k1, at + e, same(d0, d1))
            put(k2, at + e, same(d0, d2))
            put(mt, at + e, same(d0, doc_tail))
            put(mh, at + e, same(d0, doc_head))
            put(mi, at + e, same(d0, doc_in))
            put(mo, at + e, same(d0, doc_out))
            return d0, d1

        lax.fori_loop(0, XS, mask_step, (doc_at(first - 1), doc_at(first - 2)))

        fwd = [doc_at(row_first + n * TOK - 1) for n in range(PARTS + 1)]
        bwd = [doc_at(row_first + n * TOK + HALO) for n in range(PARTS + 1)]
        gone = [doc_at(row_first - k * row_span - 1) for k in range(REACH)]
        coming = [doc_at(row_first + k * row_span + HALO) for k in range(1, REACH + 1)]
        for ref, pairs in ((row_link, (fwd, bwd)), (col_link, (gone, coming))):
            for way, docs in enumerate(pairs):
                for n in range(len(docs) - 1):
                    put(ref, (which * 2 + way) * PARTS + n, same(docs[n], docs[n + 1]))


    def move(source, target, shift, c, t):
        for g in range(GROUP):
            value = source[
                c, pl.ds(pl.multiple_of(t * 16, 16), 16), g * LANES : (g + 1) * LANES
            ].astype(F32)
            target[c, pl.ds((shift + t * 16) * GROUP + g, 16, stride=GROUP), :] = value

    def relay(c, lent):
        if not lent:
            for which, (far, near_v) in enumerate(((feat, feat_v), (cot, cot_v))):
                pltpu.make_async_copy(
                    far.at[0, :, pl.ds(0, WIDTH)], near_v.at[c], load_sem.at[which, c]
                ).wait()

        def rows(t, _):
            move(feat_v, xt, HALO, c, t)
            move(cot_v, gt, 0, c, t)
            return 0

        tiles = TOK // 16
        if lent:
            lax.fori_loop(0, tiles, rows, 0)
            for n, (target, slot, row) in enumerate((
                (xt, 0, 16 - HALO), (xt, TOK + HALO, 0), (gt, TOK, 0)
            )):
                for g in range(GROUP):
                    value = rim_lent[n, :, g * LANES : (g + 1) * LANES].astype(F32)
                    target[c, pl.ds(slot * GROUP + g, HALO, stride=GROUP), :] = value[
                        row : row + HALO
                    ]
        else:
            lax.fori_loop(1, tiles - 1, rows, 0)
            move(cot_v, gt, 0, c, tiles - 1)

    def halo_set(parts, at):
        return [
            pltpu.make_async_remote_copy(
                src_ref=ref.at[parts, pl.ds(here * GROUP, HALO * GROUP), :],
                dst_ref=ref.at[parts, pl.ds(there * GROUP, HALO * GROUP), :],
                send_sem=halo_send.at[at + n],
                recv_sem=halo_recv.at[at + n],
                device_id={"seq": to},
                device_id_type=MESH,
            )
            for n, (ref, here, there, to) in enumerate((
                (xt, TOK, 0, after),
                (xt, HALO, TOK + HALO, before),
                (gt, 0, TOK, before),
            ))
        ]

    halo_copies = halo_set(pl.ds(0, LENT), 0)

    lent_cols = pl.ds(OWN, WIDTH)
    lent_tiles = pl.ds(LENT * GROUP, GROUP)
    lend_copies = [
        pltpu.make_async_remote_copy(
            src_ref=source,
            dst_ref=target,
            send_sem=lend_send.at[n],
            recv_sem=lend_recv.at[n],
            device_id={"segment": sg_to, "seq": to},
            device_id_type=MESH,
        )
        for n, (source, target, to) in enumerate((
            (ends_own, ends_lent, q),
            (taps.at[:, lent_tiles, :], tap_t.at[:, lent_tiles, :], q),
            (res.at[0, :, lent_cols], res_v.at[:, lent_cols], q),
            (rates.at[0, :, lent_cols], rates_v.at[:, lent_cols], q),
            (feat.at[0, pl.ds(TOK - 16, 16), lent_cols], rim_lent.at[0], after),
            (feat.at[0, pl.ds(0, 16), lent_cols], rim_lent.at[1], before),
            (cot.at[0, pl.ds(0, 16), lent_cols], rim_lent.at[2], before),
            (feat.at[0, :, lent_cols], feat_v.at[LENT], q),
            (cot.at[0, :, lent_cols], cot_v.at[LENT], q),
        ))
    ]

    for copy in rim:
        copy.wait()
    for c in range(LENT):
        for g in range(GROUP):
            cols = slice(c * WIDTH + g * LANES, c * WIDTH + (g + 1) * LANES)
            spread = pl.ds(HALO * GROUP + g, 16, stride=GROUP)
            xt[c, spread, :] = feat_e[0, :, cols].astype(F32)
            spread = pl.ds((HALO + TOK - 16) * GROUP + g, 16, stride=GROUP)
            xt[c, spread, :] = feat_e[1, :, cols].astype(F32)
            gt[c, pl.ds(g, 16, stride=GROUP), :] = cot_e[:, cols].astype(F32)
    across = len(three) * ((sg + last_sg) // n_sg + sg // last_sg)
    pl.semaphore_wait(barrier, (PARTS - 1) + (ROWS - 1) + 2 + across)
    for copy in halo_copies:
        copy.start()

    @pl.when(sg == last_sg)
    def _():
        for near_q in three:
            pl.semaphore_signal(
                ready, inc=1, device_id={"segment": sg_from, "seq": near_q}, device_id_type=MESH
            )

    @pl.when(sg != 0)
    def _():
        for copy in lend_copies:
            copy.start()


    def parameters(c):
        for g in range(GROUP):
            cols = slice(c * WIDTH + g * LANES, c * WIDTH + (g + 1) * LANES)
            rate = rates_v[:, cols]
            spread = pl.ds(c * STATE + g, POLES, stride=GROUP)
            dec[spread, :] = jnp.exp(-rate)
            near[spread, :] = jnp.exp(-rate * float(TOK - HALO))
            past[spread, :] = jnp.exp(-rate * float(ES))
            grow[spread, :] = jnp.exp(rate)
            dd[spread, :] = jnp.exp(-rate * float(TOK))
            dd4[spread, :] = jnp.exp(-rate * float(TOK * PARTS))
            wts[spread, :] = res_v[:, cols] * jnp.sqrt(2.0 * rate)

    masks(ends_own, 0)
    for copy in pars:
        copy.wait()
    for c in range(LENT):
        parameters(c)

    def cells(ref, at, count=CELL):
        return ref.at[pl.ds(pl.multiple_of(at * GROUP, GROUP), count * GROUP), :]

    def cell(c, who, way, pole):
        return ((c * PARTS + who) * 2 + way) * PAIR + pole

    def tail_copy(c, k):
        other = (x + k) % PARTS
        return pltpu.make_async_remote_copy(
            src_ref=cells(tails, cell(c, other, 0, 0)),
            dst_ref=cells(row_in, cell(c, x, 0, 0)),
            send_sem=tail_send.at[c, k],
            recv_sem=tail_recv.at[c, k],
            device_id={"seq": row_mate(k)},
            device_id_type=MESH,
        )

    def col_copy(c, way, k):
        slot = way * REACH + k - 1
        return pltpu.make_async_remote_copy(
            src_ref=cells(sums, (c * 2 + way) * PAIR, PAIR),
            dst_ref=cells(col_in, (c * 2 * REACH + slot) * PAIR, PAIR),
            send_sem=col_send.at[c, slot],
            recv_sem=col_recv.at[c, slot],
            device_id={"seq": col_mate(k if way == 0 else ROWS - k)},
            device_id_type=MESH,
        )

    def inc_copy(c, k):
        other = (x + k) % PARTS
        return pltpu.make_async_remote_copy(
            src_ref=cells(sent, cell(c, other, 0, 0)),
            dst_ref=cells(inc, cell(c, x, 0, 0)),
            send_sem=inc_send.at[c, k],
            recv_sem=inc_recv.at[c, k],
            device_id={"seq": row_mate(k)},
            device_id_type=MESH,
        )

    def along_row(c):
        for k in range(1, PARTS):
            tail_copy(c, k).wait_recv()
        for pole in range(PAIR):
            span = tile(dd, c * POLES + x * PAIR + pole)
            for way in range(2):
                order = list(range(PARTS)) if way == 0 else list(range(PARTS - 1, -1, -1))
                state = tile(row_in, cell(c, order[0], way, pole))
                for n in order[1:]:
                    link = tile(row_link, ((c // LENT) * 2 + way) * PARTS + n)
                    state = tile(row_in, cell(c, n, way, pole)) + link * span * state
                put(sums, (c * 2 + way) * PAIR + pole, state)
        for k in range(1, REACH + 1):
            for way in range(2):
                col_copy(c, way, k).start()

    def entering(c):
        for k in range(1, REACH + 1):
            for way in range(2):
                col_copy(c, way, k).wait_recv()
        for pole in range(PAIR):
            at = c * POLES + x * PAIR + pole
            span, long_span = tile(dd, at), tile(dd4, at)
            for way in range(2):
                slot = (c * 2 + way) * REACH
                state = tile(col_in, (slot + REACH - 1) * PAIR + pole)
                for k in range(REACH - 1, 0, -1):
                    link = tile(col_link, ((c // LENT) * 2 + way) * PARTS + k - 1)
                    state = tile(col_in, (slot + k - 1) * PAIR + pole) + link * long_span * state
                order = range(PARTS) if way == 0 else range(PARTS - 1, -1, -1)
                for n in order:
                    put(sent, cell(c, n, way, pole), state)
                    link = tile(row_link, ((c // LENT) * 2 + way) * PARTS + n)
                    state = tile(row_in, cell(c, n, way, pole)) + link * span * state
        for k in range(1, PARTS):
            inc_copy(c, k).start()
        for n in range(CELL):
            put(inc, cell(c, x, 0, n), tile(sent, cell(c, x, 0, n)))

    def xtile(c, slot):
        return xt[c, pl.ds(pl.multiple_of(slot * GROUP, GROUP), GROUP), :]

    def gtile(c, e):
        return gt[c, pl.ds(pl.multiple_of(e * GROUP, GROUP), GROUP), :]

    def first_pass(c, lent):
        relay(c, lent)
        m_at = (c // LENT) * XS
        tap = [tap_t[n, pl.ds(pl.multiple_of(c * GROUP, GROUP), GROUP), :] for n in range(9)]
        e_at = c * ES

        def stream(e, x1, x2):
            x0 = xtile(c, HALO + e)
            a, b = x1 * tile(k1, m_at + e), x2 * tile(k2, m_at + e)
            gate, key, value = (
                tap[3 * n] * x0 + tap[3 * n + 1] * a + tap[3 * n + 2] * b for n in range(3)
            )
            grad = gtile(c, e) * gate
            put(kt, e_at + e, key)
            put(vt, e_at + e, value)
            put(gft, e_at + e, grad)
            return x0, key * value, grad

        def streams(i, carry):
            x1, x2 = carry
            for u in range(6):
                x0, _, _ = stream(HALO + i * 6 + u, x1, x2)
                x1, x2 = x0, x1
            return x1, x2

        inner = TOK - HALO
        lax.fori_loop(0, inner // 6, streams, (xtile(c, HALO + 1), xtile(c, HALO)))

        decay = [tile(dec, c * POLES + p) for p in range(POLES)]

        def ends_step(i, carry):
            fwd, bwd = carry
            for u in range(3):
                e = HALO + i * 3 + u
                r = TOK - 1 - (i * 3 + u)
                mixed = tile(kt, e_at + e) * tile(vt, e_at + e) * tile(mt, m_at + e)
                grad = tile(gft, e_at + r) * tile(mh, m_at + r)
                fwd = tuple(d * s + mixed for d, s in zip(decay, fwd))
                bwd = tuple(d * s + grad for d, s in zip(decay, bwd))
            return fwd, bwd

        zero = tuple(jnp.zeros((GROUP, LANES), F32) for _ in range(POLES))
        fwd, bwd = lax.fori_loop(0, inner // 3, ends_step, (zero, zero))

        if not lent:

            @pl.when(c == 0)
            def _():
                for copy in halo_copies:
                    copy.wait_recv()

        x0, mixed0, _ = stream(0, xtile(c, 1), xtile(c, 0))
        _, mixed1, _ = stream(1, x0, xtile(c, 1))
        x0, _, grad0 = stream(TOK, xtile(c, TOK + 1), xtile(c, TOK))
        _, _, grad1 = stream(TOK + 1, x0, xtile(c, TOK + 1))
        mixed0, mixed1 = mixed0 * tile(mt, m_at), mixed1 * tile(mt, m_at + 1)
        grad0 = grad0 * tile(mh, m_at + TOK)
        grad1 = grad1 * tile(mh, m_at + TOK + 1)
        for p in range(POLES):
            far = tile(near, c * POLES + p)
            at = (c, p // PAIR)
            put(tails, cell(*at, 0, p % PAIR), fwd[p] + far * (decay[p] * mixed0 + mixed1))
            put(tails, cell(*at, 1, p % PAIR), bwd[p] + far * (decay[p] * grad1 + grad0))
        for k in range(1, PARTS):
            tail_copy(c, k).start()
        for n in range(CELL):
            put(row_in, cell(c, x, 0, n), tile(tails, cell(c, x, 0, n)))

        return 0

    def own_filters(c):
        e_at = c * ES
        m_at = (c // LENT) * XS
        decay = [tile(dec, c * POLES + p) for p in range(POLES)]
        weight = [tile(wts, c * POLES + p) for p in range(POLES)]

        def both(i, carry):
            fwd, bwd = carry
            for u in range(5):
                e = i * 5 + u
                r = ES - 1 - e
                mixed = tile(kt, e_at + e) * tile(vt, e_at + e)
                grad = tile(gft, e_at + r)
                keep, back_keep = tile(k1, m_at + e), tile(k1, m_at + r + 1)
                fwd = tuple((keep * d) * s + mixed for d, s in zip(decay, fwd))
                bwd = tuple((back_keep * d) * s + grad for d, s in zip(decay, bwd))
                put(ft, e_at + e, total_of([w * s for w, s in zip(weight, fwd)]))
                put(mx, e_at + r, total_of([w * s for w, s in zip(weight, bwd)]))
            return fwd, bwd

        zero = tuple(jnp.zeros((GROUP, LANES), F32) for _ in range(POLES))
        lax.fori_loop(0, ES // 5, both, (zero, zero))

    lax.fori_loop(0, LENT, lambda c, _: first_pass(c, False), 0)
    for copy in lend_copies[:4]:
        copy.wait_recv()
    masks(ends_lent, 1)
    parameters(LENT)
    along_row(0)

    @pl.when(sg == 0)
    def _():
        pl.semaphore_wait(ready, len(three))
        for copy in lend_copies:
            copy.start()

    for copy in lend_copies[4:]:
        copy.wait_recv()
    first_pass(LENT, True)
    along_row(1)
    own_filters(0)
    along_row(2)
    own_filters(1)
    entering(0)
    along_row(LENT)
    own_filters(2)
    entering(1)

    def out_copies(c, half):
        rows = pl.ds(pl.multiple_of(half * HALF, HALF), HALF)
        cols = pl.ds(pl.multiple_of(c * WIDTH, WIDTH), WIDTH)
        part_rows = pl.ds(pl.multiple_of(c * GROUP, GROUP), GROUP)
        scale_rows = pl.ds(pl.multiple_of((half * PARTS + c) * GROUP, GROUP), GROUP)
        return [
            pltpu.make_async_remote_copy(
                src_ref=source,
                dst_ref=target,
                send_sem=out_send.at[n, c * 2 + half],
                recv_sem=out_recv.at[n, c * 2 + half],
                device_id={"segment": sg_to},
                device_id_type=MESH,
            )
            for n, (source, target) in enumerate((
                (qv.at[c, rows, :], out_q.at[rows, cols]),
                (sv.at[scale_rows, :], (out_early, out_late)[half].at[part_rows, :]),
            ))
        ]

    def kept_copies(half):
        rows = pl.ds(half * HALF, HALF)
        scale_rows = pl.ds((half * PARTS + LENT) * GROUP, GROUP)
        return [
            pltpu.make_async_copy(
                qv.at[LENT, rows, :], out_q.at[rows, lent_cols], kept_sem.at[0, half]
            ),
            pltpu.make_async_copy(
                sv.at[scale_rows, :],
                (out_early, out_late)[half].at[lent_tiles, :],
                kept_sem.at[1, half],
            ),
        ]

    def second_pass(c, _):
        for k in range(1, PARTS):
            inc_copy(c, k).wait_recv()

        e_at = c * ES
        m_at = (c // LENT) * XS
        decay = [tile(dec, c * POLES + p) for p in range(POLES)]
        growth = [tile(grow, c * POLES + p) for p in range(POLES)]
        tap = [tap_t[n, pl.ds(pl.multiple_of(c * GROUP, GROUP), GROUP), :] for n in range(9)]

        def back_step(e, carry):
            fwd, bwd, t1, t2, t22 = carry
            key, value = tile(kt, e_at + e), tile(vt, e_at + e)
            filtered = tile(ft, e_at + e) + tile(mi, m_at + e) * total_of(fwd)
            mixed = tile(mx, e_at + e) + tile(mo, m_at + e) * total_of(bwd)
            grads = (gtile(c, e) * filtered, mixed * value, mixed * key)
            terms = [
                tap[lag] * grads[0] + tap[3 + lag] * grads[1] + tap[6 + lag] * grads[2]
                for lag in range(3)
            ]
            result = terms[0] + tile(k1, m_at + e + 1) * t1 + tile(k2, m_at + e + 2) * t22
            fwd = tuple(s * d for s, d in zip(fwd, growth))
            bwd = tuple(s * d for s, d in zip(bwd, decay))
            return result, (fwd, bwd, terms[1], terms[2], t2)

        nothing = jnp.zeros((GROUP, LANES), F32)
        fwd, bwd = [], []
        for p in range(POLES):
            weight = tile(wts, c * POLES + p)
            fwd.append(
                weight * tile(past, c * POLES + p) * tile(inc, cell(c, p // PAIR, 0, p % PAIR))
            )
            bwd.append(weight * decay[p] * tile(inc, cell(c, p // PAIR, 1, p % PAIR)))
        carry = (tuple(fwd), tuple(bwd), nothing, nothing, nothing)
        for e in (TOK + 1, TOK):
            _, carry = back_step(e, carry)

        def piece(n, carry):
            half = 1 - n
            last = half * HALF + HALF - 1

            def backward(i, inner):
                carry, most = inner
                for u in range(4):
                    e = last - (i * 4 + u)
                    result, carry = back_step(e, carry)
                    put(ot, e, result)
                    most = jnp.maximum(most, jnp.abs(result))
                return carry, most

            carry, most = lax.fori_loop(0, HALF // 4, backward, (carry, nothing))
            most = jnp.maximum(most, 1e-30)
            put(sv, half * PARTS + c, most * (1.0 / TOP))
            iv[...] = TOP / most

            def coded(i, _):
                t = half * (HALF // 16) + i
                for g in range(GROUP):
                    value = ot[pl.ds(t * 16 * GROUP + g, 16, stride=GROUP), :] * iv[g : g + 1, :]
                    qv[c, pl.ds(pl.multiple_of(t * 16, 16), 16), g * LANES : (g + 1) * LANES] = (
                        jnp.round(value).astype(jnp.int32).astype(jnp.int16)
                    )
                return 0

            lax.fori_loop(0, HALF // 16, coded, 0)

            @pl.when(c < LENT)
            def _():
                for copy in out_copies(c, half):
                    copy.start()

            @pl.when(c == LENT)
            def _():
                for copy in kept_copies(half):
                    copy.start()

            return carry

        for n in range(2):
            carry = piece(n, carry)

        @pl.when(c == 0)
        def _():
            entering(2)

        @pl.when(c == 1)
        def _():
            entering(LENT)
            own_filters(LENT)

        return 0

    lax.fori_loop(0, PARTS, second_pass, 0)

    def finish(c, _):
        for k in range(1, PARTS):
            tail_copy(c, k).wait_send()
            inc_copy(c, k).wait_send()
        for k in range(1, REACH + 1):
            for way in range(2):
                col_copy(c, way, k).wait_send()
        return 0

    def finish_out(c, _):
        for half in range(2):
            for copy in out_copies(c, half):
                copy.wait()
        return 0

    for copy in halo_copies + lend_copies:
        copy.wait_send()
    lax.fori_loop(0, PARTS, finish, 0)
    lax.fori_loop(0, LENT, finish_out, 0)
    for half in range(2):
        for copy in kept_copies(half):
            copy.wait()


def shards(features, cotangent, short_taps, residue, decay_rates, lengths):
    tokens, channels = features.shape[1:]
    far = pl.BlockSpec(memory_space=pltpu.HBM)
    bf16 = jnp.bfloat16
    vm = pltpu.VMEM
    dma = pltpu.SemaphoreType.DMA
    whole = lambda rows: vm((rows * GROUP, LANES), F32)
    coded, late, early = pl.pallas_call(
        mixer_kernel,
        out_shape=(
            jax.ShapeDtypeStruct((tokens, channels), jnp.int16),
            jax.ShapeDtypeStruct((PARTS * GROUP, LANES), F32),
            jax.ShapeDtypeStruct((PARTS * GROUP, LANES), F32),
        ),
        in_specs=[far] * 5 + [pl.BlockSpec(memory_space=pltpu.SMEM)],
        out_specs=(far, far, far),
        scratch_shapes=[
            vm((PARTS, TOK, WIDTH), bf16), vm((PARTS, TOK, WIDTH), bf16),
            vm((2, 16, channels), bf16), vm((16, channels), bf16), vm((3, 16, WIDTH), bf16),
            vm((POLES, channels), F32), vm((POLES, channels), F32),
            vm((PARTS, XS * GROUP, LANES), F32), vm((PARTS, ES * GROUP, LANES), F32),
            whole(PARTS * ES), whole(PARTS * ES), whole(PARTS * ES), whole(PARTS * ES),
            whole(PARTS * ES), whole(ES), whole(2 * XS), whole(2 * XS), whole(2 * XS),
            whole(2 * XS), whole(2 * XS), whole(2 * XS),
            vm((9, PARTS * GROUP, LANES), F32), whole(PARTS * POLES), whole(PARTS * POLES),
            whole(PARTS * POLES), whole(PARTS * POLES),
            whole(PARTS * POLES), whole(PARTS * POLES), whole(PARTS * POLES),
            whole(PARTS * 2 * POLES), whole(PARTS * 2 * POLES), whole(PARTS * CELL),
            whole(PARTS * REACH * CELL), whole(PARTS * 2 * POLES), whole(PARTS * 2 * POLES),
            whole(4 * PARTS), whole(4 * PARTS),
            vm((DOCS * GROUP, LANES), jnp.int32), vm((DOCS * GROUP, LANES), jnp.int32),
            vm((PARTS, TOK, WIDTH), jnp.int16), whole(2 * PARTS), whole(1),
            dma((2, PARTS)), dma((3,)), dma((3,)), dma((3,)),
            dma((PARTS, PARTS)), dma((PARTS, PARTS)),
            dma((PARTS, 2 * REACH)), dma((PARTS, 2 * REACH)),
            dma((PARTS, PARTS)), dma((PARTS, PARTS)), dma((2, 2 * PARTS)), dma((2, 2 * PARTS)),
            dma((3,)), dma((9,)), dma((9,)), dma((2, 2)),
            pltpu.SemaphoreType.REGULAR,
        ],
        compiler_params=pltpu.CompilerParams(
            collective_id=0, has_side_effects=True, vmem_limit_bytes=60 * 1024 * 1024
        ),
        cost_estimate=pl.CostEstimate(
            flops=160 * tokens * channels, bytes_accessed=8 * tokens * channels, transcendentals=0
        ),
    )(features, cotangent, short_taps.reshape(9, channels // LANES, LANES), residue, decay_rates, lengths)
    first_half = (jnp.arange(tokens) < HALF)[:, None]
    scale = jnp.where(first_half, early.reshape(1, channels), late.reshape(1, channels))
    return (coded.astype(F32) * scale)[None]


def solution(mesh):
    in_specs = (
        P("segment", "seq", None),
        P("segment", "seq", None),
        P("segment", None, None, None),
        P("segment", None, None),
        P("segment", None, None),
        P("segment", None),
    )
    out_specs = P("segment", "seq", None)
    return jax.shard_map(shards, mesh=mesh, in_specs=in_specs, out_specs=out_specs, check_vma=False)
```
